256 devices in a mesh: tower: 2 (over x_lo), seq: 16 (over z, core), head: 8 (over x_hi, y).
Axes of the slice: x: 4 (x_hi: 2, x_lo: 2; x = x_hi * 2 + x_lo), y: 4, z: 8, core: 2. Of those that a mesh axis runs over, the one named last changes fastest.
Arguments:
- acts: bfloat16 [2, 8192, 5, 3072], P('tower', ('seq', 'head')), may hold values from -36 to 36, as said below
- out_weight: bfloat16 [2, 3072, 3072], P('tower', 'head'), may hold values from -0.109375 to 0.109375
- pairs: int32 [2, 32, 3], P('tower', 'seq'), may hold values from -1 to 31, as said below
Outputs:
- mixed: bfloat16 [2, 8192, 3072], P('tower', ('seq', 'head'))
The draws below stay inside these ranges and needn't reach their ends.
Inputs may be any that keep to these rules, and one draw needn't show every extreme that they name: `pairs`: slot k of block i holds i - 1 + k or -1; slot 1 always holds i; block i of one tower lists j exactly where block j of the other tower lists i; some block of each tower has all three slots filled. `acts`: finite values.
All inputs are finite; a program needn't handle non-finite values.
Results may differ from the reference program's by a relative error of at most 0.018.
Values may be sent and summed in bfloat16 or wider, within the bound.
A program may use at most 128 MiB of HBM per device.

```python
import jax
import jax.numpy as jnp
from jax import lax

H = 24
DH = 128
D = 3072
TOKENS = 8192
BLK = 256
NB = 32
N_HEAD = 8


def draw_acts(key, part):
    key = jax.random.fold_in(key, 11)
    shape = (2, TOKENS, 5, D)
    scales = jnp.array([2.5, 1.0, 1.0, 1.0, 1.0], jnp.float32)[None, None, :, None]
    base = jax.random.truncated_normal(key, -4.0, 4.0, shape, jnp.float32) * scales
    return base.astype(jnp.bfloat16)


def draw_pairs(key, part):
    key = jax.random.fold_in(key, 23)
    first_key, second_key = jax.random.split(key)
    starts = jax.random.randint(first_key, (NB,), 0, 5).astype(jnp.int32)
    ends = jax.random.randint(second_key, (NB,), 0, 5).astype(jnp.int32)
    index = jnp.arange(NB, dtype=jnp.int32)
    starts = jnp.where((index == 1) | (index == 2), jnp.maximum(starts, 1), starts)
    ends = jnp.where((index == 0) | (index == 1), jnp.maximum(ends, 1), ends)
    zero = jnp.zeros((1,), jnp.int32)
    ends_before = jnp.concatenate([zero, ends[:-1]])
    starts_after = jnp.concatenate([starts[1:], zero])
    minus = jnp.full((NB,), -1, jnp.int32)
    video = jnp.stack([jnp.where(ends_before > 0, index - 1, minus), index, jnp.where(starts_after > 0, index + 1, minus)], axis=1)
    audio = jnp.stack([jnp.where((starts > 0) & (index >= 1), index - 1, minus), index, jnp.where((ends > 0) & (index < NB - 1), index + 1, minus)], axis=1)
    return jnp.stack([video, audio]).astype(jnp.int32)


def shard_levels(key, dims, cuts, smallest, high):
    def one(axis_at, parts):
        heights = jax.random.uniform(jax.random.fold_in(jax.random.fold_in(key, 6), axis_at), (parts,), jnp.float32, smallest / len(cuts), high / len(cuts))
        return jnp.repeat(jnp.exp(heights), dims[axis_at] // parts).reshape((-1,) + (1,) * (len(dims) - axis_at - 1))

    loudness = one(*cuts[0])
    for cut in cuts[1:]:
        loudness = loudness * one(*cut)
    return loudness


def bell_draw(rng, extent, scale, bound, cuts=(), kind=jnp.bfloat16):
    factor_of = shard_levels(rng, extent, cuts, -0.22, 0.18) if cuts else 1.0
    values = jax.random.normal(rng, extent, jnp.float32) * scale * factor_of
    return jnp.minimum(jnp.maximum(values, -bound), bound).astype(kind)


def setup_inputs(seed: int = 0) -> dict:
    key_list = jax.random.split(jax.random.key(seed), 4)
    acts = draw_acts(jax.random.fold_in(key_list[3], 71), 0)
    out_weight = bell_draw(key_list[1], (2, D, D), D ** -0.5, 0.109375, ((0, 2), (1, 8)))
    pairs = draw_pairs(jax.random.fold_in(key_list[3], 71), 0)
    return dict(acts=acts, out_weight=out_weight, pairs=pairs)


def soft_attend(queries, keys, values, allowed):
    scores = jnp.dot(queries.astype(jnp.float32), keys.astype(jnp.float32).T) * (DH ** -0.5)
    if allowed is not None:
        scores = jnp.where(allowed, scores, -1e30)
    peak = jnp.max(scores, axis=1, keepdims=True)
    weights = jnp.exp(scores - peak)
    if allowed is not None:
        weights = jnp.where(allowed, weights, 0.0)
    total = jnp.sum(weights, axis=1)
    mixed = jnp.dot(weights.astype(jnp.bfloat16), values, preferred_element_type=jnp.float32)
    return mixed / total[:, None]


def reference(acts, out_weight, pairs):
    width = D // N_HEAD
    outputs = []
    for tower in range(2):
        ids = pairs[tower]
        block_range = jnp.arange(NB, dtype=jnp.int32)
        block_mask = jnp.any((ids[:, :, None] == block_range[None, None, :]) & (ids[:, :, None] >= 0), axis=1)
        token_mask = jnp.repeat(jnp.repeat(block_mask, BLK, axis=0), BLK, axis=1)

        def per_head(pieces):
            query, key_self, value_self, key_cross, value_cross = pieces
            first = soft_attend(query, key_self, value_self, None)
            second = soft_attend(query, key_cross, value_cross, token_mask)
            return first + second

        def heads_of(array):
            return array.reshape(TOKENS, H, DH).transpose(1, 0, 2)

        pieces = (heads_of(acts[tower, :, 0]), heads_of(acts[tower, :, 1]), heads_of(acts[tower, :, 2]),
                  heads_of(acts[1 - tower, :, 3]), heads_of(acts[1 - tower, :, 4]))
        combined = lax.map(per_head, pieces)
        attn = combined.transpose(1, 0, 2).reshape(TOKENS, D).astype(jnp.bfloat16)
        summed = jnp.zeros((TOKENS, D), jnp.float32)
        for group in range(N_HEAD):
            part = jnp.dot(attn[:, group * width:(group + 1) * width],
                           out_weight[tower, group * width:(group + 1) * width],
                           preferred_element_type=jnp.float32).astype(jnp.bfloat16)
            part = lax.optimization_barrier(part)
            summed = summed + part.astype(jnp.float32)
        outputs.append(summed.astype(jnp.bfloat16))
    return jnp.stack(outputs)
```

```python
import functools
import math

import jax
import jax.numpy as jnp
from jax import lax
from jax.experimental import pallas as pl
from jax.experimental.pallas import tpu as pltpu
from jax.sharding import PartitionSpec as P

DH = 128
SCALE = math.log2(math.e) / math.sqrt(DH)
LOW = -1e30
LAG = 2
MESH = pl.DeviceIdType.MESH
VMEM_BYTES = 56 * 1024 * 1024


def order_of(half):
    phases = [["own"]]
    for k in range(1, half):
        before = ["sown"] if k == 1 else [f"sl{k - 1}", f"sr{k - 1}"]
        phases.append([f"l{k}", f"r{k}"] + before)
    before = ["sown"] if half == 1 else [f"sl{half - 1}", f"sr{half - 1}"]
    phases.append(["x"] + before + ["sx"])
    flat = [name for phase in phases for name in phase]
    ends = []
    for phase in phases:
        ends.append((ends[-1] if ends else 0) + len(phase))
    return {name: i for i, name in enumerate(flat)}, ends


def pick(index, values):
    result = values[0]
    for i, value in enumerate(values[1:], 1):
        result = jnp.where(index == i, value, result)
    return result


def kernel(sizes, acts, weight, pairs, out, kv, q, kvx, acc, peak, cross, attn, wv, psend, prec,
           a_send, a_recv, q_send, q_recv, x_send, x_recv, g_send, g_recv, h_send, h_recv,
           r_send, r_recv, l_sem):
    n_head, n_seq, heads, cols = sizes
    rows = acts.shape[1]
    span = rows * n_head
    blk = span // 2
    width = heads * DH
    model = out.shape[1]
    half = n_seq // 4
    place, ends = order_of(half)
    n_pos = len(place)
    n_cols = model // cols

    t, s, me = lax.axis_index("tower"), lax.axis_index("seq"), lax.axis_index("head")
    core = s % 2
    sib = s + 1 - 2 * core
    up, down = (s + 2) % n_seq, (s + n_seq - 2) % n_seq
    nxt, prv = (s + 1) % n_seq, (s + n_seq - 1) % n_seq
    far = jnp.where(core == 0, prv, nxt)

    def head_of(j):
        return (me + j) % n_head

    partners = [(t, s, head_of(j)) for j in range(1, n_head)]
    partners += [(1 - t, s, head_of(j)) for j in range(n_head)]
    partners += [(t, up, me), (t, down, me), (t, sib, me), (t, far, me)]
    barrier = pltpu.get_barrier_semaphore()
    for device in partners:
        pl.semaphore_signal(barrier, inc=1, device_id=device, device_id_type=MESH)

    def at(index, size):
        return pl.ds(pl.multiple_of(index * size, size), size)

    def remote(src, dst, send, recv, device):
        return pltpu.make_async_remote_copy(
            src_ref=src, dst_ref=dst, send_sem=send, recv_sem=recv, device_id=device, device_id_type=MESH)

    def kv_out(h, j):
        src = acts.at[pl.ds(1, 2), :, at(head_of(j) * heads + h, DH)]
        dst = kv.at[place["own"], h, :, at(me, rows), :]
        if j == 0:
            return pltpu.make_async_copy(src, dst, l_sem.at[h])
        return remote(src, dst, a_send.at[h, j], a_recv.at[h, j], (t, s, head_of(j)))

    def q_out(j):
        src, dst = acts.at[0, :, at(head_of(j), width)], q.at[at(me, rows), :]
        if j == 0:
            return pltpu.make_async_copy(src, dst, l_sem.at[heads])
        return remote(src, dst, q_send.at[j], q_recv.at[j], (t, s, head_of(j)))

    def x_out(j):
        src = acts.at[pl.ds(3, 2), :, at(head_of(j), width)]
        dst = kvx.at[:, pl.ds(pl.multiple_of(blk + me * rows, rows), rows), :]
        return remote(src, dst, x_send.at[j], x_recv.at[j], (1 - t, s, head_of(j)))

    def halo_out(way):
        src = kvx.at[:, pl.ds(2 * blk if way == 0 else blk, blk), :]
        dst = kvx.at[:, pl.ds(0 if way == 0 else 3 * blk, blk), :]
        return remote(src, dst, h_send.at[way], h_recv.at[way], (t, nxt if way == 0 else prv, me))

    def ring(h, source, target, device, part=None):
        rows_of = pl.ds(0, span) if part is None else pl.ds(part * blk, blk)
        sem = n_pos if part == 1 else place[target]
        return remote(kv.at[place[source], h, :, rows_of, :], kv.at[place[target], h, :, rows_of, :],
                      g_send.at[h, sem], g_recv.at[h, sem], device)

    def forwards(name):
        result = []
        if name[0] == "s":
            return result
        distance = 0 if name == "own" else half if name == "x" else int(name[1:])
        for way, device, part in (("l", (t, up, me), 0), ("r", (t, down, me), 1)):
            if name == "own" or name[0] == way:
                if distance + 1 < half:
                    result.append((name, f"{way}{distance + 1}", device, None))
                elif distance + 1 == half:
                    result.append((name, "x", device, part))
        result.append((name, "s" + name, (t, sib, me), None))
        return result

    def arrive(h, name):
        if name == "own":
            kv_out(h, 0).wait()
            for j in range(1, n_head):
                kv_out(h, j).wait_recv()
        elif name == "x":
            ring(h, "x", "x", (t, up, me), 0).wait_recv()
            ring(h, "x", "x", (t, down, me), 1).wait_recv()
        else:
            ring(h, name, name, (t, sib, me)).wait_recv()

    ones = jnp.ones((span, DH), jnp.bfloat16)

    def wide(value, times):
        return jnp.concatenate([value] * times, axis=1)

    def attend(h, pos):
        keys = kv[pos, h, 0]
        values = jnp.concatenate([kv[pos, h, 1], ones], axis=1)
        lanes = at(h, DH)
        for part in range(2):
            at_rows = pl.ds(part * blk, blk)
            scores = lax.dot_general(q[at_rows, lanes], keys, (((1,), (1,)), ((), ())),
                                     preferred_element_type=jnp.float32)
            old = peak[h, at_rows]
            new = jnp.maximum(old, jnp.max(scores, axis=1, keepdims=True))
            weights = jnp.exp2((scores - wide(new, span // DH)) * SCALE).astype(jnp.bfloat16)
            shrink = jnp.exp2((old - new) * SCALE)
            update = jnp.dot(weights, values, preferred_element_type=jnp.float32)
            acc[h, at_rows] = acc[h, at_rows] * wide(shrink, 2) + update
            peak[h, at_rows] = new

    def attend_cross(h, part):
        lanes = at(h, DH)
        at_rows, at_keys = at(part, blk), pl.ds(pl.multiple_of(part * blk, blk), 3 * blk)
        scores = lax.dot_general(q[at_rows, lanes], kvx[0, at_keys, lanes], (((1,), (1,)), ((), ())),
                                 preferred_element_type=jnp.float32)
        pieces = []
        for slot in range(3):
            shift = jnp.where(pairs[part, slot] >= 0, 0.0, LOW)
            pieces.append(scores[:, slot * blk:(slot + 1) * blk] + shift)
        scores = jnp.concatenate(pieces, axis=1)
        top = jnp.max(scores, axis=1, keepdims=True)
        weights = jnp.exp2((scores - top) * SCALE).astype(jnp.bfloat16)
        values = jnp.concatenate([kvx[1, at_keys, lanes], jnp.ones((3 * blk, DH), jnp.bfloat16)], axis=1)
        result = jnp.dot(weights, values, preferred_element_type=jnp.float32)
        cross[at_rows, lanes] = result[:, :DH] / result[:, DH:]

    weight_copy = pltpu.make_async_copy(weight, wv, l_sem.at[heads + 1])
    weight_copy.start()
    for h in range(heads):
        acc[h] = jnp.zeros((span, 2 * DH), jnp.float32)
        peak[h] = jnp.full((span, DH), LOW, jnp.float32)
    pl.semaphore_wait(barrier, len(partners))
    for h in range(heads):
        for j in range(n_head):
            kv_out(h, j).start()
        if h == 0:
            for j in range(n_head):
                q_out(j).start()
    for j in range(n_head):
        x_out(j).start()

    n_phases = len(ends)

    def advance(i, carry):
        tick, h = i // heads, i % heads
        phase = tick - LAG * h
        names = sorted(place, key=place.get)
        starts = [0] + ends[:-1]
        for at_phase in range(n_phases):
            @pl.when(phase == at_phase)
            def _():
                for name in names[starts[at_phase]:ends[at_phase]]:
                    arrive(h, name)
                    for hop in forwards(name):
                        ring(h, *hop).start()
                if at_phase == 0:
                    @pl.when(h == 0)
                    def _():
                        q_out(0).wait()
                        for j in range(1, n_head):
                            q_out(j).wait_recv()

        @pl.when((phase >= 0) & (phase < n_phases))
        def _():
            def step(pos, inner):
                attend(h, pos)
                return inner

            lax.fori_loop(pick(phase, starts), pick(phase, ends), step, 0)

        @pl.when((phase == 1) & (h == 0))
        def _():
            for j in range(n_head):
                x_out(j).wait_recv()
            halo_out(0).start()
            halo_out(1).start()

        @pl.when((phase == n_phases - 1) & (h == 0))
        def _():
            halo_out(0).wait_recv()
            halo_out(1).wait_recv()

            def step(index, inner):
                attend_cross(index // 2, index % 2)
                return inner

            lax.fori_loop(0, 2 * heads, step, 0)

        @pl.when(phase == n_phases - 1)
        def _():
            lanes = at(h, DH)
            self_out = acc[h, :, pl.ds(0, DH)] / acc[h, :, pl.ds(DH, DH)]
            attn[:, lanes] = (self_out + cross[:, lanes]).astype(jnp.bfloat16)

        return carry

    lax.fori_loop(0, heads * (n_phases + LAG * (heads - 1)), advance, 0)

    def share_out(n, j):
        where = at(n, cols)
        return remote(psend.at[at(head_of(j), rows), where], prec.at[j, :, where],
                      r_send.at[n, j], r_recv.at[n, j], (t, s, head_of(j)))

    weight_copy.wait()

    def project(n, carry):
        where = at(n, cols)
        psend[:, where] = jnp.dot(attn[...], wv[:, where], preferred_element_type=jnp.float32).astype(jnp.bfloat16)
        for j in range(1, n_head):
            share_out(n, j).start()
        return carry

    lax.fori_loop(0, n_cols, project, 0)

    def collect(n, carry):
        where = at(n, cols)
        total = psend[at(me, rows), where].astype(jnp.float32)
        for j in range(1, n_head):
            share_out(n, j).wait_recv()
            total = total + prec[j, :, where].astype(jnp.float32)
        out[:, where] = total.astype(jnp.bfloat16)
        return carry

    lax.fori_loop(0, n_cols, collect, 0)

    def drain(h, carry):
        for j in range(1, n_head):
            kv_out(h, j).wait_send()
        for name in place:
            for hop in forwards(name):
                ring(h, *hop).wait_send()
        return carry

    lax.fori_loop(0, heads, drain, 0)
    for j in range(n_head):
        if j:
            q_out(j).wait_send()
        x_out(j).wait_send()
    halo_out(0).wait_send()
    halo_out(1).wait_send()

    def drain_shares(n, carry):
        for j in range(1, n_head):
            share_out(n, j).wait_send()
        return carry

    lax.fori_loop(0, n_cols, drain_shares, 0)


def on_device(mesh_shape, acts, out_weight, pairs):
    n_head, n_seq = mesh_shape["head"], mesh_shape["seq"]
    rows, model = acts.shape[1], acts.shape[3]
    width = out_weight.shape[1]
    heads, span = width // DH, rows * n_head
    cols = math.gcd(model, 512)
    n_cols = model // cols
    n_pos = n_seq
    dma = pltpu.SemaphoreType.DMA
    bf16, f32 = jnp.bfloat16, jnp.float32
    result = pl.pallas_call(
        functools.partial(kernel, (n_head, n_seq, heads, cols)),
        out_shape=jax.ShapeDtypeStruct((rows, model), bf16),
        in_specs=[pl.BlockSpec(memory_space=pl.ANY), pl.BlockSpec(memory_space=pl.ANY),
                  pl.BlockSpec(memory_space=pltpu.SMEM)],
        out_specs=pl.BlockSpec(memory_space=pltpu.VMEM),
        scratch_shapes=[
            pltpu.VMEM((n_pos, heads, 2, span, DH), bf16),
            pltpu.VMEM((span, width), bf16),
            pltpu.VMEM((2, 2 * span, width), bf16),
            pltpu.VMEM((heads, span, 2 * DH), f32),
            pltpu.VMEM((heads, span, DH), f32),
            pltpu.VMEM((span, width), f32),
            pltpu.VMEM((span, width), bf16),
            pltpu.VMEM((width, model), bf16),
            pltpu.VMEM((span, model), bf16),
            pltpu.VMEM((n_head, rows, model), bf16),
            dma((heads, n_head)), dma((heads, n_head)),
            dma((n_head,)), dma((n_head,)),
            dma((n_head,)), dma((n_head,)),
            dma((heads, n_pos + 1)), dma((heads, n_pos + 1)),
            dma((2,)), dma((2,)),
            dma((n_cols, n_head)), dma((n_cols, n_head)),
            dma((heads + 2,)),
        ],
        compiler_params=pltpu.CompilerParams(
            collective_id=0, has_side_effects=True, vmem_limit_bytes=VMEM_BYTES),
        cost_estimate=pl.CostEstimate(flops=10**10, bytes_accessed=2 * 10**7, transcendentals=10**7),
    )(jnp.transpose(acts[0], (1, 0, 2)), out_weight[0], pairs[0])
    return result[None]


def solution(mesh):
    placed = (
        P("tower", ("seq", "head"), None, None),
        P("tower", "head", None),
        P("tower", "seq", None),
    )
    return jax.shard_map(
        functools.partial(on_device, dict(mesh.shape)),
        mesh=mesh,
        in_specs=placed,
        out_specs=P("tower", ("seq", "head"), None),
        check_vma=False,
    )
```

```python
import functools
import math

import jax
import jax.numpy as jnp
from jax import lax
from jax.experimental import pallas as pl
from jax.experimental.pallas import tpu as pltpu
from jax.sharding import PartitionSpec as P

DH = 128
SCALE = math.log2(math.e) / math.sqrt(DH)
LOW = -1e30
LAG = 1
N_Y = 4
MESH = pl.DeviceIdType.MESH
VMEM_BYTES = 56 * 1024 * 1024


def order_of(half):
    phases = [["own"]]
    for k in range(1, half):
        before = ["sown"] if k == 1 else [f"sl{k - 1}", f"sr{k - 1}"]
        phases.append([f"l{k}", f"r{k}"] + before)
    before = ["sown"] if half == 1 else [f"sl{half - 1}", f"sr{half - 1}"]
    phases.append(before + ["x", "sx"])
    flat = [name for phase in phases for name in phase]
    ends = []
    for phase in phases:
        ends.append((ends[-1] if ends else 0) + len(phase))
    return {name: i for i, name in enumerate(flat)}, ends


def pick(index, values):
    result = values[0]
    for i, value in enumerate(values[1:], 1):
        result = jnp.where(index == i, value, result)
    return result


def kernel(sizes, acts, weight, pairs, out, kv, q, kvx, acc, peak, cross, attn, near, wv, total, give, take,
           a_send, a_recv, q_send, q_recv, x_send, x_recv, g_send, g_recv, h_send, h_recv,
           w_send, w_recv, y_send, y_recv, r_send, r_recv, l_sem):
    n_head, n_seq, heads, cols = sizes
    rows = acts.shape[1]
    span = rows * n_head
    blk = span // 2
    width = heads * DH
    model = out.shape[1]
    half = n_seq // 4
    place, ends = order_of(half)
    n_pos = len(place)
    n_cols = model // cols

    t, s, me = lax.axis_index("tower"), lax.axis_index("seq"), lax.axis_index("head")
    core = s % 2
    sib = s + 1 - 2 * core
    up, down = (s + 2) % n_seq, (s + n_seq - 2) % n_seq
    nxt, prv = (s + 1) % n_seq, (s + n_seq - 1) % n_seq
    far = jnp.where(core == 0, prv, nxt)
    x_at, y_at = me // N_Y, me % N_Y
    w_cols = model // 2

    def head_of(j):
        return (me + j) % n_head

    partners = [(t, s, head_of(j)) for j in range(1, n_head)]
    partners += [(1 - t, s, head_of(j)) for j in range(n_head)]
    partners += [(t, up, me), (t, down, me), (t, sib, me), (t, far, me)]
    barrier = pltpu.get_barrier_semaphore()
    for device in partners:
        pl.semaphore_signal(barrier, inc=1, device_id=device, device_id_type=MESH)

    def at(index, size):
        return pl.ds(pl.multiple_of(index * size, size), size)

    def remote(src, dst, send, recv, device):
        return pltpu.make_async_remote_copy(
            src_ref=src, dst_ref=dst, send_sem=send, recv_sem=recv, device_id=device, device_id_type=MESH)

    def kv_out(h, j):
        src = acts.at[pl.ds(1, 2), :, at(head_of(j) * heads + h, DH)]
        dst = kv.at[place["own"], h, :, at(me, rows), :]
        if j == 0:
            return pltpu.make_async_copy(src, dst, l_sem.at[h])
        return remote(src, dst, a_send.at[h, j], a_recv.at[h, j], (t, s, head_of(j)))

    def q_out(j):
        src, dst = acts.at[0, :, at(head_of(j), width)], q.at[at(me, rows), :]
        if j == 0:
            return pltpu.make_async_copy(src, dst, l_sem.at[heads])
        return remote(src, dst, q_send.at[j], q_recv.at[j], (t, s, head_of(j)))

    def x_out(j):
        src = acts.at[pl.ds(3, 2), :, at(head_of(j), width)]
        dst = kvx.at[:, pl.ds(pl.multiple_of(blk + me * rows, rows), rows), :]
        return remote(src, dst, x_send.at[j], x_recv.at[j], (1 - t, s, head_of(j)))

    def halo_out(way):
        src = kvx.at[:, pl.ds(2 * blk if way == 0 else blk, blk), :]
        dst = kvx.at[:, pl.ds(0 if way == 0 else 3 * blk, blk), :]
        return remote(src, dst, h_send.at[way], h_recv.at[way], (t, nxt if way == 0 else prv, me))

    def ring(h, source, target, device, part=None):
        rows_of = pl.ds(0, span) if part is None else pl.ds(part * blk, blk)
        sem = n_pos if part == 1 else place[target]
        return remote(kv.at[place[source], h, :, rows_of, :], kv.at[place[target], h, :, rows_of, :],
                      g_send.at[h, sem], g_recv.at[h, sem], device)

    def forwards(name):
        result = []
        if name[0] == "s":
            return result
        distance = 0 if name == "own" else half if name == "x" else int(name[1:])
        for way, device, part in (("l", (t, up, me), 0), ("r", (t, down, me), 1)):
            if name == "own" or name[0] == way:
                if distance + 1 < half:
                    result.append((name, f"{way}{distance + 1}", device, None))
                elif distance + 1 == half:
                    result.append((name, "x", device, part))
        result.append((name, "s" + name, (t, sib, me), None))
        return result

    def arrive(h, name):
        if name == "own":
            kv_out(h, 0).wait()
            for j in range(1, n_head):
                kv_out(h, j).wait_recv()
        elif name == "x":
            ring(h, "x", "x", (t, up, me), 0).wait_recv()
            ring(h, "x", "x", (t, down, me), 1).wait_recv()
        else:
            ring(h, name, name, (t, sib, me)).wait_recv()

    ones = jnp.ones((span, DH), jnp.bfloat16)

    def wide(value, times):
        return jnp.concatenate([value] * times, axis=1)

    def attend(h, pos):
        keys = kv[pos, h, 0]
        values = jnp.concatenate([kv[pos, h, 1], ones], axis=1)
        lanes = at(h, DH)
        for part in range(2):
            at_rows = pl.ds(part * blk, blk)
            scores = lax.dot_general(q[at_rows, lanes], keys, (((1,), (1,)), ((), ())),
                                     preferred_element_type=jnp.float32)
            old = peak[h, at_rows]
            new = jnp.maximum(old, jnp.max(scores, axis=1, keepdims=True))
            weights = jnp.exp2((scores - wide(new, span // DH)) * SCALE).astype(jnp.bfloat16)
            shrink = jnp.exp2((old - new) * SCALE)
            update = jnp.dot(weights, values, preferred_element_type=jnp.float32)
            acc[h, at_rows] = acc[h, at_rows] * wide(shrink, 2) + update
            peak[h, at_rows] = new

    def attend_cross(h, part):
        lanes = at(h, DH)
        at_rows, at_keys = at(part, blk), pl.ds(pl.multiple_of(part * blk, blk), 3 * blk)
        scores = lax.dot_general(q[at_rows, lanes], kvx[0, at_keys, lanes], (((1,), (1,)), ((), ())),
                                 preferred_element_type=jnp.float32)
        pieces = []
        for slot in range(3):
            shift = jnp.where(pairs[part, slot] >= 0, 0.0, LOW)
            pieces.append(scores[:, slot * blk:(slot + 1) * blk] + shift)
        scores = jnp.concatenate(pieces, axis=1)
        top = jnp.max(scores, axis=1, keepdims=True)
        weights = jnp.exp2((scores - top) * SCALE).astype(jnp.bfloat16)
        values = jnp.concatenate([kvx[1, at_keys, lanes], jnp.ones((3 * blk, DH), jnp.bfloat16)], axis=1)
        result = jnp.dot(weights, values, preferred_element_type=jnp.float32)
        cross[at_rows, lanes] = result[:, :DH] / result[:, DH:]

    def along_y(j):
        return (t, s, x_at * N_Y + (y_at + j) % N_Y)

    def w_own(h):
        return pltpu.make_async_copy(weight.at[h], wv.at[h, pl.ds(0, DH)], l_sem.at[heads + 1 + h])

    def w_part(slot, owner, part=None):
        size = w_cols if part is None else w_cols // 2
        start = owner * w_cols + (0 if part is None else part * size)
        return pl.ds(slot * DH, DH), pl.ds(pl.multiple_of(start, size), size)

    def w_out(h, way):
        into, where = w_part(1 if way == 0 else N_Y - 1, core)
        return remote(weight.at[h, :, where], wv.at[h, into, where],
                      w_send.at[h, way], w_recv.at[h, way], along_y(1 if way == 0 else N_Y - 1))

    def w_on(h, way):
        rows_of, where = w_part(1 if way == 0 else N_Y - 1, core, way)
        into, unused = w_part(2, core, way)
        return remote(wv.at[h, rows_of, where], wv.at[h, into, where],
                      w_send.at[h, 2 + way], w_recv.at[h, 2 + way], along_y(1 if way == 0 else N_Y - 1))

    def w_over(h, slot, owner):
        rows_of, where = w_part(slot, owner)
        return remote(wv.at[h, rows_of, where], wv.at[h, rows_of, where],
                      w_send.at[h, 3 + slot], w_recv.at[h, 3 + slot], (t, sib, me))

    def w_first(h):
        w_own(h).start()
        w_out(h, 0).start()
        w_out(h, 1).start()

    def w_second(h):
        for way, slot in ((0, 1), (1, N_Y - 1)):
            w_out(h, way).wait_recv()
            w_on(h, way).start()
            w_over(h, slot, core).start()

    def w_third(h):
        w_on(h, 0).wait_recv()
        w_on(h, 1).wait_recv()
        w_over(h, 2, core).start()

    def attn_out(h, j):
        lanes = pl.ds(h * DH, DH)
        return remote(attn.at[:, (y_at + j) % N_Y, :, lanes], near.at[h, :, :, pl.ds(j * DH, DH)],
                      y_send.at[h, j], y_recv.at[h, j], along_y(j))

    def share_out(n):
        return remote(give.at[:, at(n, cols)], take.at[:, at(n, cols)], r_send.at[n], r_recv.at[n],
                      (t, s, (1 - x_at) * N_Y + y_at))

    def project(h):
        w_own(h).wait()
        for j in range(1, N_Y):
            attn_out(h, j).wait_recv()
            w_over(h, j, 1 - core).wait_recv()
        near[h, :, :, pl.ds(0, DH)] = attn[:, y_at, :, pl.ds(h * DH, DH)]
        mine = near[h].reshape(2 * rows, N_Y * DH)

        def step(n, carry):
            where = at(n, cols)
            value = jnp.dot(mine, wv[h, :, where], preferred_element_type=jnp.float32)
            if h:
                value = value + total[:, where]
            total[:, where] = value
            if h == heads - 1:
                give[:, where] = total[at(1 - x_at, rows), where].astype(jnp.bfloat16)
                share_out(n).start()
            return carry

        lax.fori_loop(0, n_cols, step, 0)

    def cross_of(h):
        def step(part, carry):
            attend_cross(h, part)
            return carry

        lax.fori_loop(0, 2, step, 0)

    def x_first():
        for j in range(n_head):
            x_out(j).start()

    def x_second():
        for j in range(n_head):
            x_out(j).wait_recv()
        halo_out(0).start()
        halo_out(1).start()

    def x_third():
        halo_out(0).wait_recv()
        halo_out(1).wait_recv()

    for h in range(heads):
        acc[h] = jnp.zeros((span, 2 * DH), jnp.float32)
        peak[h] = jnp.full((span, DH), LOW, jnp.float32)
    pl.semaphore_wait(barrier, len(partners))
    for h in range(heads):
        for j in range(n_head):
            kv_out(h, j).start()
        if h == 0:
            for j in range(n_head):
                q_out(j).start()
    n_phases = len(ends)
    final = heads * (n_phases - 1)
    events = [
        (min(3, final), x_first), (min(3, final + 3), lambda: w_first(0)),
        (min(6, final + 3), lambda: w_second(0)), (min(6, final + 3), lambda: w_first(1)),
        (min(7, final), x_second),
        (min(8, final + 3), lambda: w_first(2)),
        (min(9, final + 3), lambda: w_second(1)), (min(9, final + 3), lambda: w_third(0)),
        (min(10, final), x_third), (min(10, final), lambda: cross_of(0)),
        (min(11, final + 3), lambda: w_second(2)), (min(11, final + 3), lambda: w_third(1)),
        (min(13, final + 3), lambda: cross_of(1)), (min(13, final + 3), lambda: w_third(2)),
        (final + 4, lambda: project(0)), (final + 5, lambda: cross_of(2)),
        (final + 6, lambda: project(1)),
    ]

    def advance(i, carry):
        tick, h = i // heads, i % heads
        phase = tick - LAG * h
        names = sorted(place, key=place.get)
        starts = [0] + ends[:-1]
        for when in sorted({event[0] for event in events}):
            @pl.when(i == when)
            def _():
                for event in events:
                    if event[0] == when:
                        event[1]()

        for at_phase in range(n_phases - 1):
            @pl.when(phase == at_phase)
            def _():
                for name in names[starts[at_phase]:ends[at_phase]]:
                    if name[0] != "s":
                        arrive(h, name)
                        for hop in forwards(name):
                            ring(h, *hop).start()
                if at_phase == 0:
                    @pl.when(h == 0)
                    def _():
                        q_out(0).wait()
                        for j in range(1, n_head):
                            q_out(j).wait_recv()

        @pl.when((phase >= 0) & (phase < n_phases))
        def _():
            first = pick(phase, starts)
            opposite = place["x"]
            passed = first + jnp.where(phase == 0, 1, jnp.where(phase == n_phases - 1, 0, 2))

            def step(pos, inner):
                @pl.when(pos == opposite)
                def _():
                    arrive(h, "x")
                    for hop in forwards("x"):
                        ring(h, *hop).start()

                @pl.when((pos >= passed) & (pos != opposite))
                def _():
                    remote(kv.at[pos, h], kv.at[pos, h], g_send.at[h, pos], g_recv.at[h, pos], (t, sib, me)).wait_recv()

                attend(h, pos)
                return inner

            lax.fori_loop(first, pick(phase, ends), step, 0)

        for at_head in range(heads):
            @pl.when((phase == n_phases - 1) & (h == at_head))
            def _():
                lanes = pl.ds(at_head * DH, DH)
                self_out = acc[at_head, :, pl.ds(0, DH)] / acc[at_head, :, pl.ds(DH, DH)]
                value = (self_out + cross[:, lanes]).astype(jnp.bfloat16)
                attn[:, :, :, lanes] = value.reshape(2, N_Y, rows, DH)
                for j in range(1, N_Y):
                    attn_out(at_head, j).start()

        return carry

    lax.fori_loop(0, heads * (n_phases + LAG * (heads - 1)), advance, 0)
    project(heads - 1)

    def collect(n, carry):
        where = at(n, cols)
        share_out(n).wait_recv()
        out[:, where] = (total[at(x_at, rows), where] + take[:, where].astype(jnp.float32)).astype(jnp.bfloat16)
        return carry

    lax.fori_loop(0, n_cols, collect, 0)

    def drain(h, carry):
        for j in range(1, n_head):
            kv_out(h, j).wait_send()
        for name in place:
            for hop in forwards(name):
                ring(h, *hop).wait_send()
        return carry

    lax.fori_loop(0, heads, drain, 0)
    for j in range(n_head):
        if j:
            q_out(j).wait_send()
        x_out(j).wait_send()
    halo_out(0).wait_send()
    halo_out(1).wait_send()

    for h in range(heads):
        for way in range(2):
            w_out(h, way).wait_send()
            w_on(h, way).wait_send()
        for j in range(1, N_Y):
            w_over(h, j, core).wait_send()
            attn_out(h, j).wait_send()

    def drain_shares(n, carry):
        share_out(n).wait_send()
        return carry

    lax.fori_loop(0, n_cols, drain_shares, 0)


def on_device(mesh_shape, acts, out_weight, pairs):
    n_head, n_seq = mesh_shape["head"], mesh_shape["seq"]
    rows, model = acts.shape[1], acts.shape[3]
    width = out_weight.shape[1]
    heads, span = width // DH, rows * n_head
    cols = math.gcd(model, 512)
    n_cols = model // cols
    n_pos = n_seq
    dma = pltpu.SemaphoreType.DMA
    bf16, f32 = jnp.bfloat16, jnp.float32
    result = pl.pallas_call(
        functools.partial(kernel, (n_head, n_seq, heads, cols)),
        out_shape=jax.ShapeDtypeStruct((rows, model), bf16),
        in_specs=[pl.BlockSpec(memory_space=pl.ANY), pl.BlockSpec(memory_space=pl.ANY),
                  pl.BlockSpec(memory_space=pltpu.SMEM)],
        out_specs=pl.BlockSpec(memory_space=pltpu.VMEM),
        scratch_shapes=[
            pltpu.VMEM((n_pos, heads, 2, span, DH), bf16),
            pltpu.VMEM((span, width), bf16),
            pltpu.VMEM((2, 2 * span, width), bf16),
            pltpu.VMEM((heads, span, 2 * DH), f32),
            pltpu.VMEM((heads, span, DH), f32),
            pltpu.VMEM((span, width), f32),
            pltpu.VMEM((2, N_Y, rows, width), bf16),
            pltpu.VMEM((heads, 2, rows, N_Y * DH), bf16),
            pltpu.VMEM((heads, N_Y * DH, model), bf16),
            pltpu.VMEM((2 * rows, model), f32),
            pltpu.VMEM((rows, model), bf16),
            pltpu.VMEM((rows, model), bf16),
            dma((heads, n_head)), dma((heads, n_head)),
            dma((n_head,)), dma((n_head,)),
            dma((n_head,)), dma((n_head,)),
            dma((heads, n_pos + 1)), dma((heads, n_pos + 1)),
            dma((2,)), dma((2,)),
            dma((heads, 4 + N_Y)), dma((heads, 4 + N_Y)),
            dma((heads, N_Y)), dma((heads, N_Y)),
            dma((n_cols,)), dma((n_cols,)),
            dma((2 * heads + 1,)),
        ],
        compiler_params=pltpu.CompilerParams(
            collective_id=0, has_side_effects=True, vmem_limit_bytes=VMEM_BYTES),
        cost_estimate=pl.CostEstimate(flops=10**10, bytes_accessed=2 * 10**7, transcendentals=10**7),
    )(jnp.transpose(acts[0], (1, 0, 2)), out_weight[0].reshape(heads, DH, model), pairs[0])
    return result[None]


def solution(mesh):
    placed = (
        P("tower", ("seq", "head"), None, None),
        P("tower", "head", None),
        P("tower", "seq", None),
    )
    return jax.shard_map(
        functools.partial(on_device, dict(mesh.shape)),
        mesh=mesh,
        in_specs=placed,
        out_specs=P("tower", ("seq", "head"), None),
        check_vma=False,
    )
```

```python
import functools
import math

import jax
import jax.numpy as jnp
from jax import lax
from jax.experimental import pallas as pl
from jax.experimental.pallas import tpu as pltpu
from jax.sharding import PartitionSpec as P

DH = 128
SCALE = math.log2(math.e) / math.sqrt(DH)
LOW = -1e30
LAG = 1
PARTS = 2
N_Y = 4
MESH = pl.DeviceIdType.MESH
VMEM_BYTES = 56 * 1024 * 1024


def order_of(half):
    names = ["own", "sown"]
    for k in range(1, half):
        names += [f"l{k}", f"r{k}", f"sl{k}", f"sr{k}"]
    return {name: i for i, name in enumerate(names + ["x", "sx"])}


def kernel(sizes, acts, weight, pairs, out, kv, q, kvx, acc, peak, cross, attn, near, wv, total, give, take,
           a_send, a_recv, q_send, q_recv, x_send, x_recv, g_send, g_recv, o_recv, h_send, h_recv,
           w_send, w_recv, y_send, y_recv, r_send, r_recv, l_sem):
    n_head, n_seq, heads, cols = sizes
    rows = acts.shape[1]
    span = rows * n_head
    blk = span // 2
    width = heads * DH
    model = out.shape[1]
    half = n_seq // 4
    place = order_of(half)
    stops = [name for name in place if name[0] != "s"]
    n_phases = half + 1
    n_cols = model // cols

    t, s, me = lax.axis_index("tower"), lax.axis_index("seq"), lax.axis_index("head")
    core = s % 2
    sib = s + 1 - 2 * core
    up, down = (s + 2) % n_seq, (s + n_seq - 2) % n_seq
    nxt, prv = (s + 1) % n_seq, (s + n_seq - 1) % n_seq
    far = jnp.where(core == 0, prv, nxt)
    x_at, y_at = me // N_Y, me % N_Y
    w_cols = model // 2

    def head_of(j):
        return (me + j) % n_head

    partners = [(t, s, head_of(j)) for j in range(1, n_head)]
    partners += [(1 - t, s, head_of(j)) for j in range(n_head)]
    partners += [(t, up, me), (t, down, me), (t, sib, me), (t, far, me)]
    barrier = pltpu.get_barrier_semaphore()
    for device in partners:
        pl.semaphore_signal(barrier, inc=1, device_id=device, device_id_type=MESH)

    def at(index, size):
        return pl.ds(pl.multiple_of(index * size, size), size)

    def remote(src, dst, send, recv, device):
        return pltpu.make_async_remote_copy(
            src_ref=src, dst_ref=dst, send_sem=send, recv_sem=recv, device_id=device, device_id_type=MESH)

    def landed_all(ref, sem):
        pltpu.make_async_copy(ref, ref, sem).wait()

    others = pl.ds(0, span - rows)

    def kv_out(h, j):
        src = acts.at[pl.ds(1, 2), :, at(head_of(j) * heads + h, DH)]
        dst = kv.at[place["own"], h, :, at(me, rows), :]
        if j == 0:
            return pltpu.make_async_copy(src, dst, l_sem.at[h])
        return remote(src, dst, a_send.at[0], a_recv.at[h], (t, s, head_of(j)))

    def q_out(j):
        src, dst = acts.at[0, :, at(head_of(j), width)], q.at[at(me, rows), :]
        if j == 0:
            return pltpu.make_async_copy(src, dst, l_sem.at[heads])
        return remote(src, dst, q_send.at[0], q_recv.at[0], (t, s, head_of(j)))

    def x_out(j):
        src = acts.at[pl.ds(3, 2), :, at(head_of(j), width)]
        dst = kvx.at[:, pl.ds(pl.multiple_of(blk + me * rows, rows), rows), :]
        return remote(src, dst, x_send.at[0], x_recv.at[0], (1 - t, s, head_of(j)))

    def halo_out(way):
        src = kvx.at[:, pl.ds(2 * blk if way == 0 else blk, blk), :]
        dst = kvx.at[:, pl.ds(0 if way == 0 else 3 * blk, blk), :]
        return remote(src, dst, h_send.at[0], h_recv.at[way], (t, nxt if way == 0 else prv, me))

    def ring(h, source, target, device, part=None):
        rows_of = pl.ds(0, span) if part is None else pl.ds(part * blk, blk)
        if target[0] == "s":
            landed = o_recv.at[h, stops.index(target[1:])]
        else:
            landed = g_recv.at[h, stops.index(target) - 1, 0 if part is None else part]
        return remote(kv.at[place[source], h, :, rows_of, :], kv.at[place[target], h, :, rows_of, :],
                      g_send.at[0], landed, device)

    ways = {"l": (t, up, me), "r": (t, down, me)}

    def parts_of(distance):
        if distance == half:
            return {"l": [0], "r": [1]}
        whole = [None] if PARTS == 1 else [0, 1]
        return {"l": whole, "r": whole}

    def onward(name, part=None):
        distance = 0 if name == "own" else int(name[1:])
        result = []
        for way in "lr":
            if name == "own" or name[0] == way:
                for next_part in parts_of(distance + 1)[way]:
                    if part is None or next_part == part:
                        target = "x" if distance + 1 == half else f"{way}{distance + 1}"
                        result.append((name, target, ways[way], next_part))
        return result

    def over(name):
        return (name, "s" + name, (t, sib, me))

    def pass_on(h, phase):
        if phase == 0:
            kv_out(h, 0).wait()
            landed_all(kv.at[place["own"], h, :, others, :], a_recv.at[h])
            for hop in onward("own"):
                ring(h, *hop).start()
            ring(h, *over("own")).start()
        elif phase < half:
            for k in range(PARTS):
                for way in "lr":
                    parts = parts_of(phase)[way]
                    part = parts[k] if way == "l" else parts[-1 - k]
                    name = f"{way}{phase}"
                    ring(h, name, name, ways[way], part).wait_recv()
                    for hop in onward(name, part):
                        ring(h, *hop).start()
            for way in "lr":
                ring(h, *over(f"{way}{phase}")).start()
        else:
            for way, parts in parts_of(half).items():
                for part in parts:
                    ring(h, "x", "x", ways[way], part).wait_recv()
            ring(h, *over("x")).start()
        if phase > 0:
            for name in ["own"] if phase == 1 else [f"l{phase - 1}", f"r{phase - 1}"]:
                ring(h, *over(name)).wait_recv()

    def hops():
        result = onward("own") + [over("own"), over("x")]
        for k in range(1, half):
            for way in "lr":
                result += onward(f"{way}{k}") + [over(f"{way}{k}")]
        return result

    ones = jnp.ones((2 * span, DH), jnp.bfloat16)

    def wide(value, times):
        return jnp.concatenate([value] * times, axis=1)

    def attend(h, pair):
        both = pl.ds(2 * pair, 2)
        keys = kv[both, h, 0].reshape(2 * span, DH)
        values = jnp.concatenate([kv[both, h, 1].reshape(2 * span, DH), ones], axis=1)
        lanes = at(h, DH)
        parts = [pl.ds(0, blk), pl.ds(blk, blk)]
        olds = [peak[h, part] for part in parts]
        scores = [lax.dot_general(q[part, lanes], keys, (((1,), (1,)), ((), ())),
                                  preferred_element_type=jnp.float32) for part in parts]
        results = []
        for old, score in zip(olds, scores):
            new = jnp.maximum(old, jnp.max(score, axis=1, keepdims=True))
            weights = jnp.exp2((score - wide(new, 2 * span // DH)) * SCALE).astype(jnp.bfloat16)
            update = jnp.dot(weights, values, preferred_element_type=jnp.float32)
            results.append((new, jnp.exp2((old - new) * SCALE), update))
        for part, (new, shrink, update) in zip(parts, results):
            acc[h, part] = acc[h, part] * wide(shrink, 2) + update
            peak[h, part] = new

    def attend_cross(h, part):
        lanes = at(h, DH)
        at_rows, at_keys = at(part, blk), pl.ds(pl.multiple_of(part * blk, blk), 3 * blk)
        scores = lax.dot_general(q[at_rows, lanes], kvx[0, at_keys, lanes], (((1,), (1,)), ((), ())),
                                 preferred_element_type=jnp.float32)
        pieces = []
        for slot in range(3):
            shift = jnp.where(pairs[part, slot] >= 0, 0.0, LOW)
            pieces.append(scores[:, slot * blk:(slot + 1) * blk] + shift)
        scores = jnp.concatenate(pieces, axis=1)
        top = jnp.max(scores, axis=1, keepdims=True)
        weights = jnp.exp2((scores - top) * SCALE).astype(jnp.bfloat16)
        values = jnp.concatenate([kvx[1, at_keys, lanes], jnp.ones((3 * blk, DH), jnp.bfloat16)], axis=1)
        result = jnp.dot(weights, values, preferred_element_type=jnp.float32)
        cross[at_rows, lanes] = result[:, :DH] / result[:, DH:]

    def along_y(j):
        return (t, s, x_at * N_Y + (y_at + j) % N_Y)

    def w_own(h):
        return pltpu.make_async_copy(weight.at[h], wv.at[h, pl.ds(0, DH)], l_sem.at[heads + 1 + h])

    def w_part(slot, owner, part=None):
        size = w_cols if part is None else w_cols // 2
        start = owner * w_cols + (0 if part is None else part * size)
        return pl.ds(slot * DH, DH), pl.ds(pl.multiple_of(start, size), size)

    def w_out(h, way):
        into, where = w_part(1 if way == 0 else N_Y - 1, core)
        return remote(weight.at[h, :, where], wv.at[h, into, where],
                      w_send.at[0], w_recv.at[h, way], along_y(1 if way == 0 else N_Y - 1))

    def w_on(h, way):
        rows_of, where = w_part(1 if way == 0 else N_Y - 1, core, way)
        into, unused = w_part(2, core, way)
        return remote(wv.at[h, rows_of, where], wv.at[h, into, where],
                      w_send.at[0], w_recv.at[h, 2 + way], along_y(1 if way == 0 else N_Y - 1))

    def w_over(h, slot, owner):
        rows_of, where = w_part(slot, owner)
        return remote(wv.at[h, rows_of, where], wv.at[h, rows_of, where],
                      w_send.at[0], w_recv.at[h, 3 + slot], (t, sib, me))

    def w_first(h):
        w_own(h).start()
        w_out(h, 0).start()
        w_out(h, 1).start()

    def w_second(h):
        for way, slot in ((0, 1), (1, N_Y - 1)):
            w_out(h, way).wait_recv()
            w_on(h, way).start()
            w_over(h, slot, core).start()

    def w_third(h):
        w_on(h, 0).wait_recv()
        w_on(h, 1).wait_recv()
        w_over(h, 2, core).start()

    def attn_out(h, j):
        lanes = pl.ds(h * DH, DH)
        return remote(attn.at[:, (y_at + j) % N_Y, :, lanes], near.at[h, :, :, pl.ds(j * DH, DH)],
                      y_send.at[0], y_recv.at[h], along_y(j))

    def share_out(n):
        return remote(give.at[:, at(n, cols)], take.at[:, at(n, cols)], r_send.at[0], r_recv.at[n],
                      (t, s, (1 - x_at) * N_Y + y_at))

    def project(h):
        w_own(h).wait()
        for j in range(1, N_Y):
            w_over(h, j, 1 - core).wait_recv()
        landed_all(near.at[h, :, :, pl.ds(DH, (N_Y - 1) * DH)], y_recv.at[h])
        near[h, :, :, pl.ds(0, DH)] = attn[:, y_at, :, pl.ds(h * DH, DH)]
        mine = near[h].reshape(2 * rows, N_Y * DH)

        def step(n, carry):
            where = at(n, cols)
            value = jnp.dot(mine, wv[h, :, where], preferred_element_type=jnp.float32)
            if h:
                value = value + total[:, where]
            total[:, where] = value
            if h == heads - 1:
                give[:, where] = total[at(1 - x_at, rows), where].astype(jnp.bfloat16)
                share_out(n).start()
            return carry

        lax.fori_loop(0, n_cols, step, 0)

    def cross_of(h):
        def step(part, carry):
            attend_cross(h, part)
            return carry

        lax.fori_loop(0, 2, step, 0)

    def x_first():
        for j in range(n_head):
            x_out(j).start()

    def x_second():
        landed_all(kvx.at[:, pl.ds(blk, span), :], x_recv.at[0])
        halo_out(0).start()
        halo_out(1).start()

    def x_third():
        halo_out(0).wait_recv()
        halo_out(1).wait_recv()

    for h in range(heads):
        acc[h] = jnp.zeros((span, 2 * DH), jnp.float32)
        peak[h] = jnp.full((span, DH), LOW, jnp.float32)
    pl.semaphore_wait(barrier, len(partners))
    for h in range(heads):
        for j in range(n_head):
            kv_out(h, j).start()
        if h == 0:
            for j in range(n_head):
                q_out(j).start()
    final = heads * (n_phases - 1)
    late = final + 3
    events = [
        (min(3, late), lambda: w_first(0)), (min(4, late), lambda: w_first(1)), (min(5, late), lambda: w_first(2)),
        (min(5, final), x_first), (min(8, late), lambda: w_second(0)),
        (min(9, final), x_second), (min(10, late), lambda: w_second(1)),
        (min(11, final), x_third), (min(11, final), lambda: cross_of(0)),
        (min(12, late), lambda: w_second(2)), (min(12, late), lambda: w_third(0)),
        (min(12, late), lambda: cross_of(1)), (min(14, late), lambda: w_third(1)), (min(14, late), lambda: cross_of(2)),
        (min(16, late), lambda: w_third(2)), (final + 3, lambda: project(0)),
    ]

    def advance(i, carry):
        for when in sorted({event[0] for event in events}):
            @pl.when(i == when)
            def _():
                for event in events:
                    if event[0] == when:
                        event[1]()

        tick, h = i // heads, i % heads
        phase = tick - LAG * h
        for at_phase in range(n_phases):
            @pl.when(phase == at_phase)
            def _():
                pass_on(h, at_phase)

        @pl.when(i == 0)
        def _():
            q_out(0).wait()
            landed_all(q.at[others, :], q_recv.at[0])

        use(i - 1)
        return carry

    def use(i):
        tick, h = i // heads, i % heads
        phase = tick - LAG * h

        @pl.when((i >= 0) & (phase > 0) & (phase < n_phases))
        def _():
            def step(pair, inner):
                @pl.when(pair == 2 * half - 1)
                def _():
                    ring(h, *over("x")).wait_recv()

                attend(h, pair)
                return inner

            lax.fori_loop(2 * phase - 2, 2 * phase, step, 0)

        for at_head in range(heads):
            @pl.when((i >= 0) & (phase == n_phases - 1) & (h == at_head))
            def _():
                lanes = pl.ds(at_head * DH, DH)
                self_out = acc[at_head, :, pl.ds(0, DH)] / acc[at_head, :, pl.ds(DH, DH)]
                value = (self_out + cross[:, lanes]).astype(jnp.bfloat16)
                attn[:, :, :, lanes] = value.reshape(2, N_Y, rows, DH)
                for j in range(1, N_Y):
                    attn_out(at_head, j).start()

    steps = heads * (n_phases + LAG * (heads - 1))
    lax.fori_loop(0, steps, advance, 0)
    use(steps - 1)
    for h in range(1, heads):
        project(h)

    def collect(n, carry):
        where = at(n, cols)
        share_out(n).wait_recv()
        out[:, where] = (total[at(x_at, rows), where] + take[:, where].astype(jnp.float32)).astype(jnp.bfloat16)
        return carry

    lax.fori_loop(0, n_cols, collect, 0)

    landed_all(kv.at[0, :, :, others, :], a_send.at[0])
    landed_all(q.at[others, :], q_send.at[0])
    landed_all(kvx.at[:, pl.ds(0, span), :], x_send.at[0])
    landed_all(kvx.at[:, pl.ds(0, span), :], h_send.at[0])
    landed_all(kv.at[pl.ds(0, len(place) - 1)], g_send.at[0])
    landed_all(wv.at[:, pl.ds(0, (N_Y - 1) * DH), :], w_send.at[0])
    landed_all(near.at[:, :, :, pl.ds(0, (N_Y - 1) * DH)], y_send.at[0])
    landed_all(give, r_send.at[0])


def on_device(mesh_shape, acts, out_weight, pairs):
    n_head, n_seq = mesh_shape["head"], mesh_shape["seq"]
    rows, model = acts.shape[1], acts.shape[3]
    width = out_weight.shape[1]
    heads, span = width // DH, rows * n_head
    cols = math.gcd(model, 512)
    n_cols = model // cols
    n_pos = n_seq
    dma = pltpu.SemaphoreType.DMA
    bf16, f32 = jnp.bfloat16, jnp.float32
    result = pl.pallas_call(
        functools.partial(kernel, (n_head, n_seq, heads, cols)),
        out_shape=jax.ShapeDtypeStruct((rows, model), bf16),
        in_specs=[pl.BlockSpec(memory_space=pl.ANY), pl.BlockSpec(memory_space=pl.ANY),
                  pl.BlockSpec(memory_space=pltpu.SMEM)],
        out_specs=pl.BlockSpec(memory_space=pltpu.VMEM),
        scratch_shapes=[
            pltpu.VMEM((n_pos, heads, 2, span, DH), bf16),
            pltpu.VMEM((span, width), bf16),
            pltpu.VMEM((2, 2 * span, width), bf16),
            pltpu.VMEM((heads, span, 2 * DH), f32),
            pltpu.VMEM((heads, span, DH), f32),
            pltpu.VMEM((span, width), f32),
            pltpu.VMEM((2, N_Y, rows, width), bf16),
            pltpu.VMEM((heads, 2, rows, N_Y * DH), bf16),
            pltpu.VMEM((heads, N_Y * DH, model), bf16),
            pltpu.VMEM((2 * rows, model), f32),
            pltpu.VMEM((rows, model), bf16),
            pltpu.VMEM((rows, model), bf16),
            dma((1,)), dma((heads,)),
            dma((1,)), dma((1,)),
            dma((1,)), dma((1,)),
            dma((1,)), dma((heads, n_pos // 2 - 1, 2)), dma((heads, n_pos // 2)),
            dma((1,)), dma((2,)),
            dma((1,)), dma((heads, 4 + N_Y)),
            dma((1,)), dma((heads,)),
            dma((1,)), dma((n_cols,)),
            dma((2 * heads + 1,)),
        ],
        compiler_params=pltpu.CompilerParams(
            collective_id=0, has_side_effects=True, vmem_limit_bytes=VMEM_BYTES),
        cost_estimate=pl.CostEstimate(flops=10**10, bytes_accessed=2 * 10**7, transcendentals=10**7),
    )(jnp.transpose(acts[0], (1, 0, 2)), out_weight[0].reshape(heads, DH, model), pairs[0])
    return result[None]


def solution(mesh):
    placed = (
        P("tower", ("seq", "head"), None, None),
        P("tower", "head", None),
        P("tower", "seq", None),
    )
    return jax.shard_map(
        functools.partial(on_device, dict(mesh.shape)),
        mesh=mesh,
        in_specs=placed,
        out_specs=P("tower", ("seq", "head"), None),
        check_vma=False,
    )
```

```python
import functools
import math

import jax
import jax.numpy as jnp
from jax import lax
from jax.experimental import pallas as pl
from jax.experimental.pallas import tpu as pltpu
from jax.sharding import PartitionSpec as P

DH = 128
SCALE = math.log2(math.e) / math.sqrt(DH)
LOW = -1e30
PARTS = 2
N_Y = 4
MESH = pl.DeviceIdType.MESH
VMEM_BYTES = 56 * 1024 * 1024


def order_of(half):
    names = ["own", "sown"]
    for k in range(1, half):
        names += [f"l{k}", f"r{k}", f"sl{k}", f"sr{k}"]
    return {name: i for i, name in enumerate(names + ["x", "sx"])}


def kernel(sizes, acts, weight, pairs, out, kv, q, kvx, acc, peak, cross, attn, near, wv, total, give, take,
           a_send, a_recv, q_send, q_recv, x_send, x_recv, g_send, g_recv, o_recv, h_send, h_recv,
           w_send, w_recv, y_send, y_recv, r_send, r_recv, l_sem):
    n_head, n_seq, heads, cols = sizes
    rows = acts.shape[1]
    span = rows * n_head
    blk = span // 2
    width = heads * DH
    model = out.shape[1]
    half = n_seq // 4
    place = order_of(half)
    stops = [name for name in place if name[0] != "s"]
    n_phases = half + 1
    n_cols = model // cols

    t, s, me = lax.axis_index("tower"), lax.axis_index("seq"), lax.axis_index("head")
    core = s % 2
    sib = s + 1 - 2 * core
    up, down = (s + 2) % n_seq, (s + n_seq - 2) % n_seq
    nxt, prv = (s + 1) % n_seq, (s + n_seq - 1) % n_seq
    far = jnp.where(core == 0, prv, nxt)
    x_at, y_at = me // N_Y, me % N_Y
    w_cols = model // 2

    def head_of(j):
        return (me + j) % n_head

    partners = [(t, s, head_of(j)) for j in range(1, n_head)]
    partners += [(1 - t, s, head_of(j)) for j in range(n_head)]
    partners += [(t, up, me), (t, down, me), (t, sib, me), (t, far, me)]
    barrier = pltpu.get_barrier_semaphore()
    for device in partners:
        pl.semaphore_signal(barrier, inc=1, device_id=device, device_id_type=MESH)

    def at(index, size):
        return pl.ds(pl.multiple_of(index * size, size), size)

    def remote(src, dst, send, recv, device):
        return pltpu.make_async_remote_copy(
            src_ref=src, dst_ref=dst, send_sem=send, recv_sem=recv, device_id=device, device_id_type=MESH)

    def landed_all(ref, sem):
        pltpu.make_async_copy(ref, ref, sem).wait()

    others = pl.ds(0, span - rows)

    def kv_out(h, j):
        src = acts.at[pl.ds(1, 2), :, at(head_of(j) * heads + h, DH)]
        dst = kv.at[place["own"], h, :, at(me, rows), :]
        if j == 0:
            return pltpu.make_async_copy(src, dst, l_sem.at[h])
        return remote(src, dst, a_send.at[0], a_recv.at[h], (t, s, head_of(j)))

    def q_out(j):
        src, dst = acts.at[0, :, at(head_of(j), width)], q.at[at(me, rows), :]
        if j == 0:
            return pltpu.make_async_copy(src, dst, l_sem.at[heads])
        return remote(src, dst, q_send.at[0], q_recv.at[0], (t, s, head_of(j)))

    def x_out(j):
        src = acts.at[pl.ds(3, 2), :, at(head_of(j), width)]
        dst = kvx.at[:, pl.ds(pl.multiple_of(blk + me * rows, rows), rows), :]
        return remote(src, dst, x_send.at[0], x_recv.at[0], (1 - t, s, head_of(j)))

    def halo_out(way):
        src = kvx.at[:, pl.ds(2 * blk if way == 0 else blk, blk), :]
        dst = kvx.at[:, pl.ds(0 if way == 0 else 3 * blk, blk), :]
        return remote(src, dst, h_send.at[0], h_recv.at[way], (t, nxt if way == 0 else prv, me))

    def ring(h, source, target, device, part=None):
        rows_of = pl.ds(0, span) if part is None else pl.ds(part * blk, blk)
        if target[0] == "s":
            landed = o_recv.at[h, stops.index(target[1:])]
        else:
            landed = g_recv.at[h, stops.index(target) - 1, 0 if part is None else part]
        return remote(kv.at[place[source], h, :, rows_of, :], kv.at[place[target], h, :, rows_of, :],
                      g_send.at[0], landed, device)

    ways = {"l": (t, up, me), "r": (t, down, me)}

    def parts_of(distance):
        if distance == half:
            return {"l": [0], "r": [1]}
        whole = [None] if PARTS == 1 else [0, 1]
        return {"l": whole, "r": whole}

    def onward(name, part=None):
        distance = 0 if name == "own" else int(name[1:])
        result = []
        for way in "lr":
            if name == "own" or name[0] == way:
                for next_part in parts_of(distance + 1)[way]:
                    if part is None or next_part == part:
                        target = "x" if distance + 1 == half else f"{way}{distance + 1}"
                        result.append((name, target, ways[way], next_part))
        return result

    def over(name):
        return (name, "s" + name, (t, sib, me))

    def pass_on(h, phase):
        if phase == 0:
            kv_out(h, 0).wait()
            landed_all(kv.at[place["own"], h, :, others, :], a_recv.at[h])
            for hop in onward("own"):
                ring(h, *hop).start()
            ring(h, *over("own")).start()
        elif phase < half:
            for k in range(PARTS):
                for way in "lr":
                    parts = parts_of(phase)[way]
                    part = parts[k] if way == "l" else parts[-1 - k]
                    name = f"{way}{phase}"
                    ring(h, name, name, ways[way], part).wait_recv()
                    for hop in onward(name, part):
                        ring(h, *hop).start()
            for way in "lr":
                ring(h, *over(f"{way}{phase}")).start()
        else:
            for way, parts in parts_of(half).items():
                for part in parts:
                    ring(h, "x", "x", ways[way], part).wait_recv()
            ring(h, *over("x")).start()
        if 0 < phase < half:
            handed_over(h, phase)
        elif phase == half:
            @pl.when(h == 0)
            def _():
                handed_over(h, phase)

    def handed_over(h, phase):
        for name in ["own"] if phase == 1 else [f"l{phase - 1}", f"r{phase - 1}"]:
            ring(h, *over(name)).wait_recv()

    def hops():
        result = onward("own") + [over("own"), over("x")]
        for k in range(1, half):
            for way in "lr":
                result += onward(f"{way}{k}") + [over(f"{way}{k}")]
        return result

    ones = jnp.ones((2 * span, DH), jnp.bfloat16)

    def wide(value, times):
        return jnp.concatenate([value] * times, axis=1)

    def attend(blocks):
        olds, scores, values = [], [], []
        for h, pair, part in blocks:
            both = pl.ds(2 * pair, 2)
            keys = kv[both, h, 0].reshape(2 * span, DH)
            values.append(jnp.concatenate([kv[both, h, 1].reshape(2 * span, DH), ones], axis=1))
            olds.append(peak[h, part])
            scores.append(lax.dot_general(q[part, at(h, DH)], keys, (((1,), (1,)), ((), ())),
                                          preferred_element_type=jnp.float32))
        results = []
        for old, score, value in zip(olds, scores, values):
            new = jnp.maximum(old, jnp.max(score, axis=1, keepdims=True))
            weights = jnp.exp2((score - wide(new, 2 * span // DH)) * SCALE).astype(jnp.bfloat16)
            update = jnp.dot(weights, value, preferred_element_type=jnp.float32)
            results.append((new, jnp.exp2((old - new) * SCALE), update))
        for (h, pair, part), (new, shrink, update) in zip(blocks, results):
            acc[h, part] = acc[h, part] * wide(shrink, 2) + update
            peak[h, part] = new

    halves = [pl.ds(0, blk), pl.ds(blk, blk)]

    def before_last(h):
        handed_over(h, half)
        attend([(h, 2 * half - 2, part) for part in halves])

    def attend_cross(h, part):
        lanes = at(h, DH)
        at_rows, at_keys = at(part, blk), pl.ds(pl.multiple_of(part * blk, blk), 3 * blk)
        scores = lax.dot_general(q[at_rows, lanes], kvx[0, at_keys, lanes], (((1,), (1,)), ((), ())),
                                 preferred_element_type=jnp.float32)
        pieces = []
        for slot in range(3):
            shift = jnp.where(pairs[part, slot] >= 0, 0.0, LOW)
            pieces.append(scores[:, slot * blk:(slot + 1) * blk] + shift)
        scores = jnp.concatenate(pieces, axis=1)
        top = jnp.max(scores, axis=1, keepdims=True)
        weights = jnp.exp2((scores - top) * SCALE).astype(jnp.bfloat16)
        values = jnp.concatenate([kvx[1, at_keys, lanes], jnp.ones((3 * blk, DH), jnp.bfloat16)], axis=1)
        result = jnp.dot(weights, values, preferred_element_type=jnp.float32)
        cross[at_rows, lanes] = result[:, :DH] / result[:, DH:]

    def along_y(j):
        return (t, s, x_at * N_Y + (y_at + j) % N_Y)

    def w_own(h):
        return pltpu.make_async_copy(weight.at[h], wv.at[h, pl.ds(0, DH)], l_sem.at[heads + 1 + h])

    def w_part(slot, owner, part=None):
        size = w_cols if part is None else w_cols // 2
        start = owner * w_cols + (0 if part is None else part * size)
        return pl.ds(slot * DH, DH), pl.ds(pl.multiple_of(start, size), size)

    def w_out(h, way):
        into, where = w_part(1 if way == 0 else N_Y - 1, core)
        return remote(weight.at[h, :, where], wv.at[h, into, where],
                      w_send.at[0], w_recv.at[h, way], along_y(1 if way == 0 else N_Y - 1))

    def w_on(h, way):
        rows_of, where = w_part(1 if way == 0 else N_Y - 1, core, way)
        into, unused = w_part(2, core, way)
        return remote(wv.at[h, rows_of, where], wv.at[h, into, where],
                      w_send.at[0], w_recv.at[h, 2 + way], along_y(1 if way == 0 else N_Y - 1))

    def w_over(h, slot, owner):
        rows_of, where = w_part(slot, owner)
        return remote(wv.at[h, rows_of, where], wv.at[h, rows_of, where],
                      w_send.at[0], w_recv.at[h, 3 + slot], (t, sib, me))

    def w_first(h):
        w_own(h).start()
        w_out(h, 0).start()
        w_out(h, 1).start()

    def w_second(h):
        for way, slot in ((0, 1), (1, N_Y - 1)):
            w_out(h, way).wait_recv()
            w_on(h, way).start()
            w_over(h, slot, core).start()

    def w_third(h):
        w_on(h, 0).wait_recv()
        w_on(h, 1).wait_recv()
        w_over(h, 2, core).start()

    def attn_out(h, home, j):
        return remote(attn.at[home, (y_at + j) % N_Y, :, pl.ds(h * DH, DH)], near.at[h, home, :, pl.ds(j * DH, DH)],
                      y_send.at[0], y_recv.at[h, home], along_y(j))

    def finish(h, home):
        part, lanes = at(home, blk), pl.ds(h * DH, DH)
        self_out = acc[h, part, pl.ds(0, DH)] / acc[h, part, pl.ds(DH, DH)]
        value = (self_out + cross[part, lanes]).astype(jnp.bfloat16)
        attn[home, :, :, lanes] = value.reshape(N_Y, rows, DH)
        for j in range(1, N_Y):
            attn_out(h, home, j).start()

    def gathered(h, home):
        landed_all(near.at[h, home, :, pl.ds(DH, (N_Y - 1) * DH)], y_recv.at[h, home])
        near[h, home, :, pl.ds(0, DH)] = attn[home, y_at, :, pl.ds(h * DH, DH)]

    def weights_here(h):
        w_own(h).wait()
        for j in range(1, N_Y):
            w_over(h, j, 1 - core).wait_recv()

    def share_out(n):
        return remote(give.at[:, at(n, cols)], take.at[:, at(n, cols)], r_send.at[0], r_recv.at[n],
                      (t, s, (1 - x_at) * N_Y + y_at))

    def project_first():
        weights_here(0)
        gathered(0, 0)
        gathered(0, 1)
        mine = near[0].reshape(2 * rows, N_Y * DH)

        def step(n, carry):
            where = at(n, cols)
            total[:, where] = jnp.dot(mine, wv[0, :, where], preferred_element_type=jnp.float32)
            return carry

        lax.fori_loop(0, n_cols, step, 0)

    def project_late(home, send):
        for h in range(1, heads):
            if send:
                weights_here(h)
            gathered(h, home)
        mine = [near[h, home] for h in range(1, heads)]

        def step(n, carry):
            where = at(n, cols)
            value = total[at(home, rows), where]
            for h in range(1, heads):
                value += jnp.dot(mine[h - 1], wv[h, :, where], preferred_element_type=jnp.float32)
            if send:
                give[:, where] = value.astype(jnp.bfloat16)
                share_out(n).start()
            else:
                total[at(home, rows), where] = value
            return carry

        lax.fori_loop(0, n_cols, step, 0)

    def cross_of(h):
        def step(part, carry):
            attend_cross(h, part)
            return carry

        lax.fori_loop(0, 2, step, 0)

    def x_first():
        for j in range(n_head):
            x_out(j).start()

    def x_second():
        landed_all(kvx.at[:, pl.ds(blk, span), :], x_recv.at[0])
        halo_out(0).start()
        halo_out(1).start()

    def x_third():
        halo_out(0).wait_recv()
        halo_out(1).wait_recv()

    for h in range(heads):
        acc[h] = jnp.zeros((span, 2 * DH), jnp.float32)
        peak[h] = jnp.full((span, DH), LOW, jnp.float32)
    pl.semaphore_wait(barrier, len(partners))
    for h in range(heads):
        for j in range(n_head):
            kv_out(h, j).start()
        if h == 0:
            for j in range(n_head):
                q_out(j).start()
    final = heads * (n_phases - 1)
    late = final + 3
    events = [
        (min(5, final), x_first), (min(3, late), lambda: w_first(0)),
        (min(4, late), lambda: w_first(1)), (min(5, late), lambda: w_first(2)),
        (min(9, final), x_second), (min(8, late), lambda: w_second(0)),
        (min(11, final), x_third), (min(11, final), lambda: cross_of(0)),
        (min(10, late), lambda: w_second(1)), (min(12, late), lambda: cross_of(1)),
        (min(13, late), lambda: cross_of(2)), (min(12, late), lambda: w_second(2)),
        (min(12, late), lambda: w_third(0)), (min(14, late), lambda: w_third(1)), (min(16, late), lambda: w_third(2)),
    ]

    def advance(i, carry):
        for when in sorted({event[0] for event in events}):
            @pl.when(i == when)
            def _():
                for event in events:
                    if event[0] == when:
                        event[1]()

        tick, h = i // heads, i % heads
        phase = tick - jnp.where(h == 0, 0, 1)
        for at_phase in range(n_phases):
            @pl.when(phase == at_phase)
            def _():
                pass_on(h, at_phase)

        @pl.when(i == 0)
        def _():
            q_out(0).wait()
            landed_all(q.at[others, :], q_recv.at[0])

        use(i - 1)
        return carry

    def use(i):
        tick, h = i // heads, i % heads
        phase = tick - jnp.where(h == 0, 0, 1)

        @pl.when((i >= 0) & (phase > 0) & (phase < jnp.where(h == 0, n_phases, n_phases - 1)))
        def _():
            def step(pair, inner):
                @pl.when(pair == 2 * half - 1)
                def _():
                    ring(h, *over("x")).wait_recv()

                attend([(h, pair, part) for part in halves])
                return inner

            lax.fori_loop(2 * phase - 2, 2 * phase, step, 0)

        @pl.when((i >= 0) & (phase == n_phases - 1) & (h == 0))
        def _():
            finish(0, 0)
            finish(0, 1)

    steps = heads * (n_phases + 1)
    lax.fori_loop(0, steps, advance, 0)
    use(steps - 1)

    late_heads = range(1, heads)
    for h in late_heads:
        before_last(h)
    for h in late_heads:
        ring(h, *over("x")).wait_recv()
    for home in (1 - x_at, x_at):
        attend([(h, 2 * half - 1, at(home, blk)) for h in late_heads])
        for h in late_heads:
            finish(h, home)
    project_first()
    project_late(1 - x_at, True)
    project_late(x_at, False)

    def collect(n, carry):
        where = at(n, cols)
        share_out(n).wait_recv()
        out[:, where] = (total[at(x_at, rows), where] + take[:, where].astype(jnp.float32)).astype(jnp.bfloat16)
        return carry

    lax.fori_loop(0, n_cols, collect, 0)

    landed_all(kv.at[0, :, :, others, :], a_send.at[0])
    landed_all(q.at[others, :], q_send.at[0])
    landed_all(kvx.at[:, pl.ds(0, span), :], x_send.at[0])
    landed_all(kvx.at[:, pl.ds(0, span), :], h_send.at[0])
    landed_all(kv.at[pl.ds(0, len(place) - 1)], g_send.at[0])
    landed_all(wv.at[:, pl.ds(0, (N_Y - 1) * DH), :], w_send.at[0])
    landed_all(near.at[:, :, :, pl.ds(0, (N_Y - 1) * DH)], y_send.at[0])
    landed_all(give, r_send.at[0])


def on_device(mesh_shape, acts, out_weight, pairs):
    n_head, n_seq = mesh_shape["head"], mesh_shape["seq"]
    rows, model = acts.shape[1], acts.shape[3]
    width = out_weight.shape[1]
    heads, span = width // DH, rows * n_head
    cols = math.gcd(model, 512)
    n_cols = model // cols
    n_pos = n_seq
    dma = pltpu.SemaphoreType.DMA
    bf16, f32 = jnp.bfloat16, jnp.float32
    result = pl.pallas_call(
        functools.partial(kernel, (n_head, n_seq, heads, cols)),
        out_shape=jax.ShapeDtypeStruct((rows, model), bf16),
        in_specs=[pl.BlockSpec(memory_space=pl.ANY), pl.BlockSpec(memory_space=pl.ANY),
                  pl.BlockSpec(memory_space=pltpu.SMEM)],
        out_specs=pl.BlockSpec(memory_space=pltpu.VMEM),
        scratch_shapes=[
            pltpu.VMEM((n_pos, heads, 2, span, DH), bf16),
            pltpu.VMEM((span, width), bf16),
            pltpu.VMEM((2, 2 * span, width), bf16),
            pltpu.VMEM((heads, span, 2 * DH), f32),
            pltpu.VMEM((heads, span, DH), f32),
            pltpu.VMEM((span, width), f32),
            pltpu.VMEM((2, N_Y, rows, width), bf16),
            pltpu.VMEM((heads, 2, rows, N_Y * DH), bf16),
            pltpu.VMEM((heads, N_Y * DH, model), bf16),
            pltpu.VMEM((2 * rows, model), f32),
            pltpu.VMEM((rows, model), bf16),
            pltpu.VMEM((rows, model), bf16),
            dma((1,)), dma((heads,)),
            dma((1,)), dma((1,)),
            dma((1,)), dma((1,)),
            dma((1,)), dma((heads, n_pos // 2 - 1, 2)), dma((heads, n_pos // 2)),
            dma((1,)), dma((2,)),
            dma((1,)), dma((heads, 4 + N_Y)),
            dma((1,)), dma((heads, 2)),
            dma((1,)), dma((n_cols,)),
            dma((2 * heads + 1,)),
        ],
        compiler_params=pltpu.CompilerParams(
            collective_id=0, has_side_effects=True, vmem_limit_bytes=VMEM_BYTES),
        cost_estimate=pl.CostEstimate(flops=10**10, bytes_accessed=2 * 10**7, transcendentals=10**7),
    )(jnp.transpose(acts[0], (1, 0, 2)), out_weight[0].reshape(heads, DH, model), pairs[0])
    return result[None]


def solution(mesh):
    placed = (
        P("tower", ("seq", "head"), None, None),
        P("tower", "head", None),
        P("tower", "seq", None),
    )
    return jax.shard_map(
        functools.partial(on_device, dict(mesh.shape)),
        mesh=mesh,
        in_specs=placed,
        out_specs=P("tower", ("seq", "head"), None),
        check_vma=False,
    )
```

```python
import functools
import math

import jax
import jax.numpy as jnp
from jax import lax
from jax.experimental import pallas as pl
from jax.experimental.pallas import tpu as pltpu
from jax.sharding import PartitionSpec as P

DH = 128
SCALE = math.log2(math.e) / math.sqrt(DH)
LOW = -1e30
PARTS = 2
N_Y = 4
MESH = pl.DeviceIdType.MESH
VMEM_BYTES = 56 * 1024 * 1024


def order_of(half):
    names = ["own", "sown"]
    for k in range(1, half):
        names += [f"l{k}", f"r{k}", f"sl{k}", f"sr{k}"]
    return {name: i for i, name in enumerate(names + ["x", "sx"])}


def kernel(sizes, acts, weight, pairs, out, kv, q, kvx, acc, peak, cross, attn, near, wv, total, give, take, done,
           a_send, a_recv, q_send, q_recv, x_send, x_recv, g_send, g_recv, o_recv, h_send, h_recv,
           w_send, w_recv, y_send, y_recv, r_send, r_recv, l_sem, d_sem):
    n_head, n_seq, heads, cols = sizes
    rows = acts.shape[1]
    span = rows * n_head
    blk = span // 2
    width = heads * DH
    model = out.shape[1]
    half = n_seq // 4
    place = order_of(half)
    stops = [name for name in place if name[0] != "s"]
    n_phases = half + 1
    n_cols = model // cols

    t, s, me = lax.axis_index("tower"), lax.axis_index("seq"), lax.axis_index("head")
    core = s % 2
    sib = s + 1 - 2 * core
    up, down = (s + 2) % n_seq, (s + n_seq - 2) % n_seq
    nxt, prv = (s + 1) % n_seq, (s + n_seq - 1) % n_seq
    far = jnp.where(core == 0, prv, nxt)
    x_at, y_at = me // N_Y, me % N_Y
    w_cols = model // 2

    def head_of(j):
        return (me + j) % n_head

    partners = [(t, up, me), (t, down, me), (t, far, me), (t, sib, me)]
    partners += [(t, s, head_of(j)) for j in range(1, n_head)]
    partners += [(1 - t, s, head_of(j)) for j in range(n_head)]
    barrier = pltpu.get_barrier_semaphore()
    for device in partners:
        pl.semaphore_signal(barrier, inc=1, device_id=device, device_id_type=MESH)

    def at(index, size):
        return pl.ds(pl.multiple_of(index * size, size), size)

    def remote(src, dst, send, recv, device):
        return pltpu.make_async_remote_copy(
            src_ref=src, dst_ref=dst, send_sem=send, recv_sem=recv, device_id=device, device_id_type=MESH)

    def landed_all(ref, sem):
        pltpu.make_async_copy(ref, ref, sem).wait()

    others = pl.ds(0, span - rows)

    def kv_out(h, j):
        src = acts.at[pl.ds(1, 2), :, at(head_of(j) * heads + h, DH)]
        dst = kv.at[place["own"], h, :, at(me, rows), :]
        if j == 0:
            return pltpu.make_async_copy(src, dst, l_sem.at[h])
        return remote(src, dst, a_send.at[0], a_recv.at[h], (t, s, head_of(j)))

    def q_out(j):
        src, dst = acts.at[0, :, at(head_of(j), width)], q.at[at(me, rows), :]
        if j == 0:
            return pltpu.make_async_copy(src, dst, l_sem.at[heads])
        return remote(src, dst, q_send.at[0], q_recv.at[0], (t, s, head_of(j)))

    def x_out(j):
        src = acts.at[pl.ds(3, 2), :, at(head_of(j), width)]
        dst = kvx.at[:, pl.ds(pl.multiple_of(blk + me * rows, rows), rows), :]
        return remote(src, dst, x_send.at[0], x_recv.at[0], (1 - t, s, head_of(j)))

    def halo_out(way):
        src = kvx.at[:, pl.ds(2 * blk if way == 0 else blk, blk), :]
        dst = kvx.at[:, pl.ds(0 if way == 0 else 3 * blk, blk), :]
        return remote(src, dst, h_send.at[0], h_recv.at[way], (t, nxt if way == 0 else prv, me))

    def ring(h, source, target, device, part=None):
        rows_of = pl.ds(0, span) if part is None else pl.ds(part * blk, blk)
        if target[0] == "s":
            landed = o_recv.at[h, stops.index(target[1:]) + (part or 0)]
        else:
            landed = g_recv.at[h, stops.index(target) - 1, 0 if part is None else part]
        return remote(kv.at[place[source], h, :, rows_of, :], kv.at[place[target], h, :, rows_of, :],
                      g_send.at[0], landed, device)

    ways = {"l": (t, up, me), "r": (t, down, me)}

    def parts_of(distance):
        if distance == half:
            return {"l": [0], "r": [1]}
        whole = [None] if PARTS == 1 else [0, 1]
        return {"l": whole, "r": whole}

    def onward(name, part=None):
        distance = 0 if name == "own" else int(name[1:])
        result = []
        for way in "lr":
            if name == "own" or name[0] == way:
                for next_part in parts_of(distance + 1)[way]:
                    if part is None or next_part == part:
                        target = "x" if distance + 1 == half else f"{way}{distance + 1}"
                        result.append((name, target, ways[way], next_part))
        return result

    def over(name):
        return (name, "s" + name, (t, sib, me))

    def pass_on(h, phase):
        if phase == 0:
            kv_out(h, 0).wait()
            landed_all(kv.at[place["own"], h, :, others, :], a_recv.at[h])
            left, right = [[hop for hop in onward("own") if hop[2] is ways[way]] for way in "lr"]
            for pair in zip(left, right[::-1]):
                for hop in pair:
                    ring(h, *hop).start()
            ring(h, *over("own")).start()
        elif phase < half:
            for k in range(PARTS):
                for way in "lr":
                    parts = parts_of(phase)[way]
                    part = parts[k] if way == "l" else parts[-1 - k]
                    name = f"{way}{phase}"
                    ring(h, name, name, ways[way], part).wait_recv()
                    for hop in onward(name, part):
                        ring(h, *hop).start()
            for way in "lr":
                ring(h, *over(f"{way}{phase}")).start()
        else:
            for way, parts in parts_of(half).items():
                for part in parts:
                    ring(h, "x", "x", ways[way], part).wait_recv()
                    ring(h, *over("x"), part).start()
        if 0 < phase < half:
            handed_over(h, phase)
        elif phase == half:
            @pl.when(h == 0)
            def _():
                handed_over(h, phase)

    def handed_over(h, phase):
        for name in ["own"] if phase == 1 else [f"l{phase - 1}", f"r{phase - 1}"]:
            ring(h, *over(name)).wait_recv()

    def hops():
        result = onward("own") + [over("own"), over("x")]
        for k in range(1, half):
            for way in "lr":
                result += onward(f"{way}{k}") + [over(f"{way}{k}")]
        return result

    ones = jnp.ones((2 * span, DH), jnp.bfloat16)

    def wide(value, times):
        return jnp.concatenate([value] * times, axis=1)

    def attend(blocks):
        olds, scores, values = [], [], []
        for h, pair, part in blocks:
            both = pl.ds(2 * pair, 2)
            keys = kv[both, h, 0].reshape(2 * span, DH)
            values.append(jnp.concatenate([kv[both, h, 1].reshape(2 * span, DH), ones], axis=1))
            olds.append(peak[h, part])
            scores.append(lax.dot_general(q[part, at(h, DH)], keys, (((1,), (1,)), ((), ())),
                                          preferred_element_type=jnp.float32))
        results = []
        for old, score, value in zip(olds, scores, values):
            new = jnp.maximum(old, jnp.max(score, axis=1, keepdims=True))
            weights = jnp.exp2((score - wide(new, 2 * span // DH)) * SCALE).astype(jnp.bfloat16)
            update = jnp.dot(weights, value, preferred_element_type=jnp.float32)
            results.append((new, jnp.exp2((old - new) * SCALE), update))
        for (h, pair, part), (new, shrink, update) in zip(blocks, results):
            acc[h, part] = acc[h, part] * wide(shrink, 2) + update
            peak[h, part] = new

    halves = [pl.ds(0, blk), pl.ds(blk, blk)]

    def before_last(h):
        handed_over(h, half)
        attend([(h, 2 * half - 2, part) for part in halves])

    def attend_cross(h, part):
        lanes = at(h, DH)
        at_rows, at_keys = at(part, blk), pl.ds(pl.multiple_of(part * blk, blk), 3 * blk)
        scores = lax.dot_general(q[at_rows, lanes], kvx[0, at_keys, lanes], (((1,), (1,)), ((), ())),
                                 preferred_element_type=jnp.float32)
        pieces = []
        for slot in range(3):
            shift = jnp.where(pairs[part, slot] >= 0, 0.0, LOW)
            pieces.append(scores[:, slot * blk:(slot + 1) * blk] + shift)
        scores = jnp.concatenate(pieces, axis=1)
        top = jnp.max(scores, axis=1, keepdims=True)
        weights = jnp.exp2((scores - top) * SCALE).astype(jnp.bfloat16)
        values = jnp.concatenate([kvx[1, at_keys, lanes], jnp.ones((3 * blk, DH), jnp.bfloat16)], axis=1)
        result = jnp.dot(weights, values, preferred_element_type=jnp.float32)
        cross[at_rows, lanes] = result[:, :DH] / result[:, DH:]

    def along_y(j):
        return (t, s, x_at * N_Y + (y_at + j) % N_Y)

    def w_own(h):
        return pltpu.make_async_copy(weight.at[h], wv.at[h, pl.ds(0, DH)], l_sem.at[heads + 1 + h])

    def w_part(slot, owner, part=None):
        size = w_cols if part is None else w_cols // 2
        start = owner * w_cols + (0 if part is None else part * size)
        return pl.ds(slot * DH, DH), pl.ds(pl.multiple_of(start, size), size)

    def w_out(h, way):
        into, where = w_part(1 if way == 0 else N_Y - 1, core)
        return remote(weight.at[h, :, where], wv.at[h, into, where],
                      w_send.at[0], w_recv.at[h, way], along_y(1 if way == 0 else N_Y - 1))

    def w_on(h, way):
        rows_of, where = w_part(1 if way == 0 else N_Y - 1, core, way)
        into, unused = w_part(2, core, way)
        return remote(wv.at[h, rows_of, where], wv.at[h, into, where],
                      w_send.at[0], w_recv.at[h, 2 + way], along_y(1 if way == 0 else N_Y - 1))

    def w_over(h, slot, owner):
        rows_of, where = w_part(slot, owner)
        return remote(wv.at[h, rows_of, where], wv.at[h, rows_of, where],
                      w_send.at[0], w_recv.at[h, 3 + slot], (t, sib, me))

    def w_first(h):
        w_own(h).start()
        w_out(h, 0).start()
        w_out(h, 1).start()

    def w_second(h):
        for way, slot in ((0, 1), (1, N_Y - 1)):
            w_out(h, way).wait_recv()
            w_on(h, way).start()
            w_over(h, slot, core).start()

    def w_third(h):
        w_on(h, 0).wait_recv()
        w_on(h, 1).wait_recv()
        w_over(h, 2, core).start()

    def attn_out(h, home, j):
        return remote(attn.at[home, (y_at + j) % N_Y, :, pl.ds(h * DH, DH)], near.at[h, home, :, pl.ds(j * DH, DH)],
                      y_send.at[0], y_recv.at[h, home], along_y(j))

    def finish(h, home):
        part, lanes = at(home, blk), pl.ds(h * DH, DH)
        self_out = acc[h, part, pl.ds(0, DH)] / acc[h, part, pl.ds(DH, DH)]
        value = (self_out + cross[part, lanes]).astype(jnp.bfloat16)
        attn[home, :, :, lanes] = value.reshape(N_Y, rows, DH)
        for j in range(1, N_Y):
            attn_out(h, home, j).start()

    def gathered(h, home):
        landed_all(near.at[h, home, :, pl.ds(DH, (N_Y - 1) * DH)], y_recv.at[h, home])
        near[h, home, :, pl.ds(0, DH)] = attn[home, y_at, :, pl.ds(h * DH, DH)]

    def weights_here(h):
        w_own(h).wait()
        for j in range(1, N_Y):
            w_over(h, j, 1 - core).wait_recv()

    def share_out(n):
        return remote(give.at[:, at(n, cols)], take.at[:, at(n, cols)], r_send.at[0], r_recv.at[n],
                      (t, s, (1 - x_at) * N_Y + y_at))

    def project_first():
        weights_here(0)
        gathered(0, 0)
        gathered(0, 1)
        mine = near[0].reshape(2 * rows, N_Y * DH)

        def step(n, carry):
            where = at(n, cols)
            total[:, where] = jnp.dot(mine, wv[0, :, where], preferred_element_type=jnp.float32)
            return carry

        lax.fori_loop(0, n_cols, step, 0)

    def project_late(home, send):
        for h in range(1, heads):
            if send:
                weights_here(h)
            gathered(h, home)
        mine = [near[h, home] for h in range(1, heads)]

        def step(n, carry):
            where = at(n, cols)
            value = total[at(home, rows), where]
            for h in range(1, heads):
                value += jnp.dot(mine[h - 1], wv[h, :, where], preferred_element_type=jnp.float32)
            if send:
                give[:, where] = value.astype(jnp.bfloat16)
                share_out(n).start()
            else:
                total[at(home, rows), where] = value
            return carry

        lax.fori_loop(0, n_cols, step, 0)

    def cross_of(h):
        def step(part, carry):
            attend_cross(h, part)
            return carry

        lax.fori_loop(0, 2, step, 0)

    def x_first():
        for j in range(n_head):
            x_out(j).start()

    def x_second():
        landed_all(kvx.at[:, pl.ds(blk, span), :], x_recv.at[0])
        halo_out(0).start()
        halo_out(1).start()

    def x_third():
        halo_out(0).wait_recv()
        halo_out(1).wait_recv()

    for h in range(heads):
        acc[h] = jnp.zeros((span, 2 * DH), jnp.float32)
        peak[h] = jnp.full((span, DH), LOW, jnp.float32)
    pl.semaphore_wait(barrier, len(partners))
    for h in range(heads):
        for j in range(n_head):
            kv_out(h, j).start()
        if h == 0:
            for j in range(n_head):
                q_out(j).start()
    final = heads * (n_phases - 1)
    late = final + 3
    events = [
        (min(5, final), x_first), (min(3, late), lambda: w_first(0)),
        (min(4, late), lambda: w_first(1)), (min(5, late), lambda: w_first(2)),
        (min(9, final), x_second), (min(8, late), lambda: w_second(0)),
        (min(12, final), x_third), (min(12, final), lambda: cross_of(0)),
        (min(10, late), lambda: w_second(1)), (min(13, late), lambda: cross_of(1)),
        (min(14, late), lambda: cross_of(2)), (min(12, late), lambda: w_second(2)),
        (min(12, late), lambda: w_third(0)), (min(14, late), lambda: w_third(1)), (min(16, late), lambda: w_third(2)),
    ]

    def advance(i, carry):
        for when in sorted({event[0] for event in events}):
            @pl.when(i == when)
            def _():
                for event in events:
                    if event[0] == when:
                        event[1]()

        tick, h = i // heads, i % heads
        phase = tick - jnp.where(h == 0, 0, 1)
        for at_phase in range(n_phases):
            @pl.when(phase == at_phase)
            def _():
                pass_on(h, at_phase)

        @pl.when(i == 0)
        def _():
            q_out(0).wait()
            landed_all(q.at[others, :], q_recv.at[0])

        use(i - 1)
        return carry

    def use(i):
        tick, h = i // heads, i % heads
        phase = tick - jnp.where(h == 0, 0, 1)

        @pl.when((i >= 0) & (phase > 0) & (phase < jnp.where(h == 0, n_phases, n_phases - 1)))
        def _():
            def step(pair, inner):
                @pl.when(pair == 2 * half - 1)
                def _():
                    for part in range(2):
                        ring(h, *over("x"), part).wait_recv()

                attend([(h, pair, part) for part in halves])
                return inner

            lax.fori_loop(2 * phase - 2, 2 * phase, step, 0)

        @pl.when((i >= 0) & (phase == n_phases - 1) & (h == 0))
        def _():
            finish(0, 0)
            finish(0, 1)

    steps = heads * (n_phases + 1)
    lax.fori_loop(0, steps, advance, 0)
    use(steps - 1)

    late_heads = range(1, heads)
    for h in late_heads:
        before_last(h)
    for h in late_heads:
        for part in range(2):
            ring(h, *over("x"), part).wait_recv()
    for home in (1 - x_at, x_at):
        attend([(h, 2 * half - 1, at(home, blk)) for h in late_heads])
        for h in late_heads:
            finish(h, home)
    project_first()
    project_late(1 - x_at, True)
    project_late(x_at, False)

    def collect(n, carry):
        where = at(n, cols)
        share_out(n).wait_recv()
        done[:, where] = (total[at(x_at, rows), where] + take[:, where].astype(jnp.float32)).astype(jnp.bfloat16)
        pltpu.make_async_copy(done.at[:, where], out.at[:, where], d_sem.at[0]).start()
        return carry

    lax.fori_loop(0, n_cols, collect, 0)

    landed_all(done, d_sem.at[0])

    landed_all(kv.at[0, :, :, others, :], a_send.at[0])
    landed_all(q.at[others, :], q_send.at[0])
    landed_all(kvx.at[:, pl.ds(0, span), :], x_send.at[0])
    landed_all(kvx.at[:, pl.ds(0, span), :], h_send.at[0])
    landed_all(kv.at[pl.ds(0, len(place) - 1)], g_send.at[0])
    landed_all(wv.at[:, pl.ds(0, (N_Y - 1) * DH), :], w_send.at[0])
    landed_all(near.at[:, :, :, pl.ds(0, (N_Y - 1) * DH)], y_send.at[0])
    landed_all(give, r_send.at[0])


def on_device(mesh_shape, acts, out_weight, pairs):
    n_head, n_seq = mesh_shape["head"], mesh_shape["seq"]
    rows, model = acts.shape[1], acts.shape[3]
    width = out_weight.shape[1]
    heads, span = width // DH, rows * n_head
    cols = math.gcd(model, 512)
    n_cols = model // cols
    n_pos = n_seq
    dma = pltpu.SemaphoreType.DMA
    bf16, f32 = jnp.bfloat16, jnp.float32
    result = pl.pallas_call(
        functools.partial(kernel, (n_head, n_seq, heads, cols)),
        out_shape=jax.ShapeDtypeStruct((rows, model), bf16),
        in_specs=[pl.BlockSpec(memory_space=pl.ANY), pl.BlockSpec(memory_space=pl.ANY),
                  pl.BlockSpec(memory_space=pltpu.SMEM)],
        out_specs=pl.BlockSpec(memory_space=pl.ANY),
        scratch_shapes=[
            pltpu.VMEM((n_pos, heads, 2, span, DH), bf16),
            pltpu.VMEM((span, width), bf16),
            pltpu.VMEM((2, 2 * span, width), bf16),
            pltpu.VMEM((heads, span, 2 * DH), f32),
            pltpu.VMEM((heads, span, DH), f32),
            pltpu.VMEM((span, width), f32),
            pltpu.VMEM((2, N_Y, rows, width), bf16),
            pltpu.VMEM((heads, 2, rows, N_Y * DH), bf16),
            pltpu.VMEM((heads, N_Y * DH, model), bf16),
            pltpu.VMEM((2 * rows, model), f32),
            pltpu.VMEM((rows, model), bf16),
            pltpu.VMEM((rows, model), bf16),
            pltpu.VMEM((rows, model), bf16),
            dma((1,)), dma((heads,)),
            dma((1,)), dma((1,)),
            dma((1,)), dma((1,)),
            dma((1,)), dma((heads, n_pos // 2 - 1, 2)), dma((heads, n_pos // 2 + 1)),
            dma((1,)), dma((2,)),
            dma((1,)), dma((heads, 4 + N_Y)),
            dma((1,)), dma((heads, 2)),
            dma((1,)), dma((n_cols,)),
            dma((2 * heads + 1,)), dma((1,)),
        ],
        compiler_params=pltpu.CompilerParams(
            collective_id=0, has_side_effects=True, vmem_limit_bytes=VMEM_BYTES),
        cost_estimate=pl.CostEstimate(flops=10**10, bytes_accessed=2 * 10**7, transcendentals=10**7),
    )(jnp.transpose(acts[0], (1, 0, 2)), out_weight[0].reshape(heads, DH, model), pairs[0])
    return result[None]


def solution(mesh):
    placed = (
        P("tower", ("seq", "head"), None, None),
        P("tower", "head", None),
        P("tower", "seq", None),
    )
    return jax.shard_map(
        functools.partial(on_device, dict(mesh.shape)),
        mesh=mesh,
        in_specs=placed,
        out_specs=P("tower", ("seq", "head"), None),
        check_vma=False,
    )
```

```python
import functools
import math

import jax
import jax.numpy as jnp
from jax import lax
from jax.experimental import pallas as pl
from jax.experimental.pallas import tpu as pltpu
from jax.sharding import PartitionSpec as P

DH = 128
SCALE = math.log2(math.e) / math.sqrt(DH)
LOW = -1e30
PARTS = 2
N_Y = 4
MESH = pl.DeviceIdType.MESH
VMEM_BYTES = 56 * 1024 * 1024


def order_of(half):
    names = ["own", "sown"]
    for k in range(1, half):
        names += [f"l{k}", f"r{k}", f"sl{k}", f"sr{k}"]
    return {name: i for i, name in enumerate(names + ["x", "sx"])}


def kernel(sizes, acts, weight, pairs, out, kv, q, kvx, acc, peak, cross, attn, near, wv, total, give, take, done,
           a_send, a_recv, q_send, q_recv, x_send, x_recv, g_send, g_recv, o_recv, h_send, h_recv,
           w_send, w_recv, y_send, y_recv, r_send, r_recv, l_sem, d_sem):
    n_head, n_seq, heads, cols = sizes
    rows = acts.shape[1]
    span = rows * n_head
    blk = span // 2
    width = heads * DH
    model = out.shape[1]
    half = n_seq // 4
    place = order_of(half)
    stops = [name for name in place if name[0] != "s"]
    n_phases = half + 1
    n_cols = model // cols

    t, s, me = lax.axis_index("tower"), lax.axis_index("seq"), lax.axis_index("head")
    core = s % 2
    sib = s + 1 - 2 * core
    up, down = (s + 2) % n_seq, (s + n_seq - 2) % n_seq
    nxt, prv = (s + 1) % n_seq, (s + n_seq - 1) % n_seq
    far = jnp.where(core == 0, prv, nxt)
    x_at, y_at = me // N_Y, me % N_Y
    w_cols = model // 2

    def head_of(j):
        return (me + j) % n_head

    partners = [(t, up, me), (t, down, me), (t, far, me), (t, sib, me)]
    partners += [(t, s, head_of(j)) for j in range(1, n_head)]
    partners += [(1 - t, s, head_of(j)) for j in range(n_head)]
    barrier = pltpu.get_barrier_semaphore()
    for device in partners:
        pl.semaphore_signal(barrier, inc=1, device_id=device, device_id_type=MESH)

    def at(index, size):
        return pl.ds(pl.multiple_of(index * size, size), size)

    def remote(src, dst, send, recv, device):
        return pltpu.make_async_remote_copy(
            src_ref=src, dst_ref=dst, send_sem=send, recv_sem=recv, device_id=device, device_id_type=MESH)

    def landed_all(ref, sem):
        pltpu.make_async_copy(ref, ref, sem).wait()

    others = pl.ds(0, span - rows)

    def kv_out(h, j):
        src = acts.at[pl.ds(1, 2), :, at(head_of(j) * heads + h, DH)]
        dst = kv.at[place["own"], h, :, at(me, rows), :]
        if j == 0:
            return pltpu.make_async_copy(src, dst, l_sem.at[h])
        return remote(src, dst, a_send.at[0], a_recv.at[h], (t, s, head_of(j)))

    def q_out(j):
        src, dst = acts.at[0, :, at(head_of(j), width)], q.at[at(me, rows), :]
        if j == 0:
            return pltpu.make_async_copy(src, dst, l_sem.at[heads])
        return remote(src, dst, q_send.at[0], q_recv.at[0], (t, s, head_of(j)))

    def x_out(j):
        src = acts.at[pl.ds(3, 2), :, at(head_of(j), width)]
        dst = kvx.at[:, pl.ds(pl.multiple_of(blk + me * rows, rows), rows), :]
        return remote(src, dst, x_send.at[0], x_recv.at[0], (1 - t, s, head_of(j)))

    def halo_out(way):
        src = kvx.at[:, pl.ds(2 * blk if way == 0 else blk, blk), :]
        dst = kvx.at[:, pl.ds(0 if way == 0 else 3 * blk, blk), :]
        return remote(src, dst, h_send.at[0], h_recv.at[way], (t, nxt if way == 0 else prv, me))

    def ring(h, source, target, device, part=None):
        rows_of = pl.ds(0, span) if part is None else pl.ds(part * blk, blk)
        if target[0] == "s":
            landed = o_recv.at[h, stops.index(target[1:]) + (part or 0)]
        else:
            landed = g_recv.at[h, stops.index(target) - 1, 0 if part is None else part]
        return remote(kv.at[place[source], h, :, rows_of, :], kv.at[place[target], h, :, rows_of, :],
                      g_send.at[0], landed, device)

    ways = {"l": (t, up, me), "r": (t, down, me)}

    def parts_of(distance):
        if distance == half:
            return {"l": [0], "r": [1]}
        whole = [None] if PARTS == 1 else [0, 1]
        return {"l": whole, "r": whole}

    def onward(name, part=None):
        distance = 0 if name == "own" else int(name[1:])
        result = []
        for way in "lr":
            if name == "own" or name[0] == way:
                for next_part in parts_of(distance + 1)[way]:
                    if part is None or next_part == part:
                        target = "x" if distance + 1 == half else f"{way}{distance + 1}"
                        result.append((name, target, ways[way], next_part))
        return result

    def over(name):
        return (name, "s" + name, (t, sib, me))

    def pass_on(h, phase):
        if phase == 0:
            kv_out(h, 0).wait()
            landed_all(kv.at[place["own"], h, :, others, :], a_recv.at[h])
            left, right = [[hop for hop in onward("own") if hop[2] is ways[way]] for way in "lr"]
            for pair in zip(left, right[::-1]):
                for hop in pair:
                    ring(h, *hop).start()
            ring(h, *over("own")).start()
        elif phase < half:
            for k in range(PARTS):
                for way in "lr":
                    parts = parts_of(phase)[way]
                    part = parts[k] if way == "l" else parts[-1 - k]
                    name = f"{way}{phase}"
                    ring(h, name, name, ways[way], part).wait_recv()
                    for hop in onward(name, part):
                        ring(h, *hop).start()
            for way in "lr":
                ring(h, *over(f"{way}{phase}")).start()
        else:
            for way, parts in parts_of(half).items():
                for part in parts:
                    ring(h, "x", "x", ways[way], part).wait_recv()
                    ring(h, *over("x"), part).start()
        if 0 < phase < half:
            handed_over(h, phase)
        elif phase == half:
            @pl.when(h == 0)
            def _():
                handed_over(h, phase)

    def handed_over(h, phase):
        for name in ["own"] if phase == 1 else [f"l{phase - 1}", f"r{phase - 1}"]:
            ring(h, *over(name)).wait_recv()

    def hops():
        result = onward("own") + [over("own"), over("x")]
        for k in range(1, half):
            for way in "lr":
                result += onward(f"{way}{k}") + [over(f"{way}{k}")]
        return result

    ones = jnp.ones((2 * span, DH), jnp.bfloat16)

    def wide(value, times):
        return jnp.concatenate([value] * times, axis=1)

    def attend(blocks):
        olds, scores, values = [], [], []
        for h, pair, part in blocks:
            both = pl.ds(2 * pair, 2)
            keys = kv[both, h, 0].reshape(2 * span, DH)
            values.append(jnp.concatenate([kv[both, h, 1].reshape(2 * span, DH), ones], axis=1))
            olds.append(peak[h, part])
            scores.append(lax.dot_general(q[part, at(h, DH)], keys, (((1,), (1,)), ((), ())),
                                          preferred_element_type=jnp.float32))
        results = []
        for old, score, value in zip(olds, scores, values):
            new = jnp.maximum(old, jnp.max(score, axis=1, keepdims=True))
            weights = jnp.exp2((score - wide(new, 2 * span // DH)) * SCALE).astype(jnp.bfloat16)
            update = jnp.dot(weights, value, preferred_element_type=jnp.float32)
            results.append((new, jnp.exp2((old - new) * SCALE), update))
        for (h, pair, part), (new, shrink, update) in zip(blocks, results):
            acc[h, part] = acc[h, part] * wide(shrink, 2) + update
            peak[h, part] = new

    halves = [pl.ds(0, blk), pl.ds(blk, blk)]

    def before_last(h):
        handed_over(h, half)
        attend([(h, 2 * half - 2, part) for part in halves])

    def attend_cross(h, part):
        lanes = at(h, DH)
        at_rows, at_keys = at(part, blk), pl.ds(pl.multiple_of(part * blk, blk), 3 * blk)
        scores = lax.dot_general(q[at_rows, lanes], kvx[0, at_keys, lanes], (((1,), (1,)), ((), ())),
                                 preferred_element_type=jnp.float32)
        pieces = []
        for slot in range(3):
            shift = jnp.where(pairs[part, slot] >= 0, 0.0, LOW)
            pieces.append(scores[:, slot * blk:(slot + 1) * blk] + shift)
        scores = jnp.concatenate(pieces, axis=1)
        top = jnp.max(scores, axis=1, keepdims=True)
        weights = jnp.exp2((scores - top) * SCALE).astype(jnp.bfloat16)
        values = jnp.concatenate([kvx[1, at_keys, lanes], jnp.ones((3 * blk, DH), jnp.bfloat16)], axis=1)
        result = jnp.dot(weights, values, preferred_element_type=jnp.float32)
        cross[at_rows, lanes] = result[:, :DH] / result[:, DH:]

    def along_y(j):
        return (t, s, x_at * N_Y + (y_at + j) % N_Y)

    def w_own(h):
        return pltpu.make_async_copy(weight.at[h], wv.at[h, pl.ds(0, DH)], l_sem.at[heads + 1 + h])

    def w_part(slot, owner, part=None):
        size = w_cols if part is None else w_cols // 2
        start = owner * w_cols + (0 if part is None else part * size)
        return pl.ds(slot * DH, DH), pl.ds(pl.multiple_of(start, size), size)

    def w_out(h, way):
        into, where = w_part(1 if way == 0 else N_Y - 1, core)
        return remote(weight.at[h, :, where], wv.at[h, into, where],
                      w_send.at[0], w_recv.at[h, way], along_y(1 if way == 0 else N_Y - 1))

    def w_on(h, way):
        rows_of, where = w_part(1 if way == 0 else N_Y - 1, core, way)
        into, unused = w_part(2, core, way)
        return remote(wv.at[h, rows_of, where], wv.at[h, into, where],
                      w_send.at[0], w_recv.at[h, 2 + way], along_y(1 if way == 0 else N_Y - 1))

    def w_over(h, slot, owner):
        rows_of, where = w_part(slot, owner)
        return remote(wv.at[h, rows_of, where], wv.at[h, rows_of, where],
                      w_send.at[0], w_recv.at[h, 3 + slot], (t, sib, me))

    def w_first(h):
        w_own(h).start()
        w_out(h, 0).start()
        w_out(h, 1).start()

    def w_second(h):
        for way, slot in ((0, 1), (1, N_Y - 1)):
            w_out(h, way).wait_recv()
            w_on(h, way).start()
            w_over(h, slot, core).start()

    def w_third(h):
        w_on(h, 0).wait_recv()
        w_on(h, 1).wait_recv()
        w_over(h, 2, core).start()

    def attn_out(h, home, j):
        return remote(attn.at[home, (y_at + j) % N_Y, :, pl.ds(h * DH, DH)], near.at[h, home, :, pl.ds(j * DH, DH)],
                      y_send.at[0], y_recv.at[h, home], along_y(j))

    def finish(h, home):
        part, lanes = at(home, blk), pl.ds(h * DH, DH)
        self_out = acc[h, part, pl.ds(0, DH)] / acc[h, part, pl.ds(DH, DH)]
        value = (self_out + cross[part, lanes]).astype(jnp.bfloat16)
        attn[home, :, :, lanes] = value.reshape(N_Y, rows, DH)
        for j in range(1, N_Y):
            attn_out(h, home, j).start()

    def gathered(h, home):
        landed_all(near.at[h, home, :, pl.ds(DH, (N_Y - 1) * DH)], y_recv.at[h, home])
        near[h, home, :, pl.ds(0, DH)] = attn[home, y_at, :, pl.ds(h * DH, DH)]

    def weights_here(h):
        w_own(h).wait()
        for j in range(1, N_Y):
            w_over(h, j, 1 - core).wait_recv()

    def share_out(n):
        return remote(give.at[:, at(n, cols)], take.at[:, at(n, cols)], r_send.at[0], r_recv.at[n],
                      (t, s, (1 - x_at) * N_Y + y_at))

    def project_first():
        weights_here(0)
        gathered(0, 0)
        gathered(0, 1)
        mine = near[0].reshape(2 * rows, N_Y * DH)

        def step(n, carry):
            where = at(n, cols)
            total[:, where] = jnp.dot(mine, wv[0, :, where], preferred_element_type=jnp.float32)
            return carry

        lax.fori_loop(0, n_cols, step, 0)

    def project_late(home, send):
        for h in range(1, heads):
            if send:
                weights_here(h)
            gathered(h, home)
        mine = [near[h, home] for h in range(1, heads)]

        def step(n, carry):
            where = at(n, cols)
            value = total[at(home, rows), where]
            for h in range(1, heads):
                value += jnp.dot(mine[h - 1], wv[h, :, where], preferred_element_type=jnp.float32)
            if send:
                give[:, where] = value.astype(jnp.bfloat16)
                share_out(n).start()
            else:
                total[at(home, rows), where] = value
            return carry

        lax.fori_loop(0, n_cols, step, 0)

    def cross_of(h):
        def step(part, carry):
            attend_cross(h, part)
            return carry

        lax.fori_loop(0, 2, step, 0)

    def x_first():
        for j in range(n_head):
            x_out(j).start()

    def x_second():
        landed_all(kvx.at[:, pl.ds(blk, span), :], x_recv.at[0])
        halo_out(0).start()
        halo_out(1).start()

    def x_third():
        halo_out(0).wait_recv()
        halo_out(1).wait_recv()

    for h in range(heads):
        acc[h] = jnp.zeros((span, 2 * DH), jnp.float32)
        peak[h] = jnp.full((span, DH), LOW, jnp.float32)
    pl.semaphore_wait(barrier, len(partners))
    for h in range(heads):
        for j in sorted(range(n_head), key=lambda j: -min(j % N_Y, N_Y - j % N_Y)):
            kv_out(h, j).start()
        if h == 0:
            for j in range(n_head):
                q_out(j).start()
    final = heads * (n_phases - 1)
    late = final + 3
    events = [
        (min(5, final), x_first), (min(3, late), lambda: w_first(0)),
        (min(4, late), lambda: w_first(1)), (min(5, late), lambda: w_first(2)),
        (min(9, final), x_second), (min(8, late), lambda: w_second(0)),
        (min(12, final), x_third), (min(12, final), lambda: cross_of(0)),
        (min(10, late), lambda: w_second(1)), (min(13, late), lambda: cross_of(1)),
        (min(14, late), lambda: cross_of(2)), (min(12, late), lambda: w_second(2)),
        (min(12, late), lambda: w_third(0)), (min(14, late), lambda: w_third(1)), (min(16, late), lambda: w_third(2)),
    ]

    def advance(i, carry):
        for when in sorted({event[0] for event in events}):
            @pl.when(i == when)
            def _():
                for event in events:
                    if event[0] == when:
                        event[1]()

        tick, h = i // heads, i % heads
        phase = tick - jnp.where(h == 0, 0, 1)
        for at_phase in range(n_phases):
            @pl.when(phase == at_phase)
            def _():
                pass_on(h, at_phase)

        @pl.when(i == 0)
        def _():
            q_out(0).wait()
            landed_all(q.at[others, :], q_recv.at[0])

        use(i - 1)
        return carry

    def use(i):
        tick, h = i // heads, i % heads
        phase = tick - jnp.where(h == 0, 0, 1)

        @pl.when((i >= 0) & (phase > 0) & (phase < jnp.where(h == 0, n_phases, n_phases - 1)))
        def _():
            def step(pair, inner):
                @pl.when(pair == 2 * half - 1)
                def _():
                    for part in range(2):
                        ring(h, *over("x"), part).wait_recv()

                attend([(h, pair, part) for part in halves])
                return inner

            lax.fori_loop(2 * phase - 2, 2 * phase, step, 0)

        @pl.when((i >= 0) & (phase == n_phases - 1) & (h == 0))
        def _():
            finish(0, 0)
            finish(0, 1)

    steps = heads * (n_phases + 1)
    lax.fori_loop(0, steps, advance, 0)
    use(steps - 1)

    late_heads = range(1, heads)
    for h in late_heads:
        before_last(h)
    for h in late_heads:
        for part in range(2):
            ring(h, *over("x"), part).wait_recv()
    for home in (1 - x_at, x_at):
        attend([(h, 2 * half - 1, at(home, blk)) for h in late_heads])
        for h in late_heads:
            finish(h, home)
    project_first()
    project_late(1 - x_at, True)
    project_late(x_at, False)

    def collect(n, carry):
        where = at(n, cols)
        share_out(n).wait_recv()
        done[:, where] = (total[at(x_at, rows), where] + take[:, where].astype(jnp.float32)).astype(jnp.bfloat16)
        pltpu.make_async_copy(done.at[:, where], out.at[:, where], d_sem.at[0]).start()
        return carry

    lax.fori_loop(0, n_cols, collect, 0)

    landed_all(done, d_sem.at[0])

    landed_all(kv.at[0, :, :, others, :], a_send.at[0])
    landed_all(q.at[others, :], q_send.at[0])
    landed_all(kvx.at[:, pl.ds(0, span), :], x_send.at[0])
    landed_all(kvx.at[:, pl.ds(0, span), :], h_send.at[0])
    landed_all(kv.at[pl.ds(0, len(place) - 1)], g_send.at[0])
    landed_all(wv.at[:, pl.ds(0, (N_Y - 1) * DH), :], w_send.at[0])
    landed_all(near.at[:, :, :, pl.ds(0, (N_Y - 1) * DH)], y_send.at[0])
    landed_all(give, r_send.at[0])


def on_device(mesh_shape, acts, out_weight, pairs):
    n_head, n_seq = mesh_shape["head"], mesh_shape["seq"]
    rows, model = acts.shape[1], acts.shape[3]
    width = out_weight.shape[1]
    heads, span = width // DH, rows * n_head
    cols = math.gcd(model, 512)
    n_cols = model // cols
    n_pos = n_seq
    dma = pltpu.SemaphoreType.DMA
    bf16, f32 = jnp.bfloat16, jnp.float32
    result = pl.pallas_call(
        functools.partial(kernel, (n_head, n_seq, heads, cols)),
        out_shape=jax.ShapeDtypeStruct((rows, model), bf16),
        in_specs=[pl.BlockSpec(memory_space=pl.ANY), pl.BlockSpec(memory_space=pl.ANY),
                  pl.BlockSpec(memory_space=pltpu.SMEM)],
        out_specs=pl.BlockSpec(memory_space=pl.ANY),
        scratch_shapes=[
            pltpu.VMEM((n_pos, heads, 2, span, DH), bf16),
            pltpu.VMEM((span, width), bf16),
            pltpu.VMEM((2, 2 * span, width), bf16),
            pltpu.VMEM((heads, span, 2 * DH), f32),
            pltpu.VMEM((heads, span, DH), f32),
            pltpu.VMEM((span, width), f32),
            pltpu.VMEM((2, N_Y, rows, width), bf16),
            pltpu.VMEM((heads, 2, rows, N_Y * DH), bf16),
            pltpu.VMEM((heads, N_Y * DH, model), bf16),
            pltpu.VMEM((2 * rows, model), f32),
            pltpu.VMEM((rows, model), bf16),
            pltpu.VMEM((rows, model), bf16),
            pltpu.VMEM((rows, model), bf16),
            dma((1,)), dma((heads,)),
            dma((1,)), dma((1,)),
            dma((1,)), dma((1,)),
            dma((1,)), dma((heads, n_pos // 2 - 1, 2)), dma((heads, n_pos // 2 + 1)),
            dma((1,)), dma((2,)),
            dma((1,)), dma((heads, 4 + N_Y)),
            dma((1,)), dma((heads, 2)),
            dma((1,)), dma((n_cols,)),
            dma((2 * heads + 1,)), dma((1,)),
        ],
        compiler_params=pltpu.CompilerParams(
            collective_id=0, has_side_effects=True, vmem_limit_bytes=VMEM_BYTES),
        cost_estimate=pl.CostEstimate(flops=10**10, bytes_accessed=2 * 10**7, transcendentals=10**7),
    )(jnp.transpose(acts[0], (1, 0, 2)), out_weight[0].reshape(heads, DH, model), pairs[0])
    return result[None]


def solution(mesh):
    placed = (
        P("tower", ("seq", "head"), None, None),
        P("tower", "head", None),
        P("tower", "seq", None),
    )
    return jax.shard_map(
        functools.partial(on_device, dict(mesh.shape)),
        mesh=mesh,
        in_specs=placed,
        out_specs=P("tower", ("seq", "head"), None),
        check_vma=False,
    )
```
